128 devices in a mesh: replica: 8 (over x_lo, z), fsdp: 16 (over x_hi, y, core).
Axes of the slice: x: 4 (x_hi: 2, x_lo: 2; x = x_hi * 2 + x_lo), y: 4, z: 4, core: 2. Of those that a mesh axis runs over, the one named last changes fastest.
Arguments:
- queries: bfloat16 [32768, 2048], P(('replica', 'fsdp')), may hold values from -6 to 6
- keys: bfloat16 [32768, 2048], P(('replica', 'fsdp')), may hold values from -6 to 6
- values: bfloat16 [32768, 2048], P(('replica', 'fsdp')), may hold values from -6 to 6
- log_decay: float32 [16, 32768], P(None, ('replica', 'fsdp')), may hold values from -1 to 0, as said below
- write_strength: float32 [16, 32768], P(None, ('replica', 'fsdp')), may hold values from 0.1 to 1
- out_grad: bfloat16 [32768, 4096], P(('replica', 'fsdp')), may hold values from -6 to 6
- replica_weights: float32 [8, 2048, 4096], P('replica', 'fsdp'), may hold values from -8 to 8
- adam_first: float32 [8, 2048, 4096], P('replica', 'fsdp'), may hold values from -1.5 to 1.5
- adam_second: float32 [8, 2048, 4096], P('replica', 'fsdp'), may hold values from 0.05 to 0.5
- anchor: float32 [2048, 4096], P('fsdp'), may hold values from -6 to 6
- outer_momentum: float32 [2048, 4096], P('fsdp'), may hold values from -0.3125 to 0.3125
- exponents: int32 [8, 16], P('replica', 'fsdp'), may hold values from -13 to -11
Outputs:
- layer_out: bfloat16 [32768, 4096], P(('replica', 'fsdp'))
- new_anchor: float32 [2048, 4096], P('fsdp')
- new_momentum: float32 [2048, 4096], P('fsdp')
The draws below stay inside these ranges and needn't reach their ends.
Inputs may be any that keep to these rules, and one draw needn't show every extreme that they name: `log_decay`: negative.
All inputs are finite; a program needn't handle non-finite values.
Results may differ from the reference program's by a relative error of at most 0.0057.
Values may be sent and summed in bfloat16 or wider, within the bound.
A program may use at most 128 MiB of HBM per device.

```python
import math
import jax
import jax.numpy as jnp
from jax import lax

D = 4096
OWNED_ATTN_UNITS = 16
HEAD = 128
BLOCK = 128
POSITIONS_PER_GPU = 256
HV = 2048
TOKENS = 32768
BLOCKS = 16
N_REPLICA = 8
N_FSDP = 16


def draw_log_decay(key, part):
    key = jax.random.fold_in(key, 5)
    first_key, second_key, prng_partition_part, fourth_key = jax.random.split(key, 4)
    number_of_batches = TOKENS // POSITIONS_PER_GPU
    lowest = math.log(1.0 / (20.0 * POSITIONS_PER_GPU))
    highest = math.log(1.0 / 30.0)
    stepsize_factor = jnp.exp(jax.random.uniform(first_key, (OWNED_ATTN_UNITS, number_of_batches, 1), jnp.float32, lowest, highest))
    random_perturbation = jax.random.uniform(second_key, (OWNED_ATTN_UNITS, number_of_batches, POSITIONS_PER_GPU), jnp.float32, 0.5, 2.0)
    spike_occurrences = jax.random.uniform(prng_partition_part, (OWNED_ATTN_UNITS, number_of_batches, POSITIONS_PER_GPU), jnp.float32) < 3.0 / POSITIONS_PER_GPU
    kept_matrix_lines = jax.random.uniform(fourth_key, (OWNED_ATTN_UNITS, number_of_batches, POSITIONS_PER_GPU), jnp.float32, 0.5, 0.8)
    payload_matrix_lines = -stepsize_factor * random_perturbation + jnp.where(spike_occurrences, jnp.log(kept_matrix_lines), 0.0)
    return payload_matrix_lines.reshape(OWNED_ATTN_UNITS, TOKENS).astype(jnp.float32)


def shared_anchor(key):
    base_key = jax.random.fold_in(key, 11)
    return jnp.clip(jax.random.normal(base_key, (HV, D), jnp.float32), -6.0, 6.0)


def draw_anchor(key, part):
    return shared_anchor(key)


def draw_replica_weights(key, part):
    base = shared_anchor(key)
    key = jax.random.fold_in(key, 7)
    first_key, second_key, prng_partition_part = jax.random.split(key, 3)
    row_scale = jnp.exp(jax.random.uniform(first_key, (N_REPLICA, HV, 1), jnp.float32, 0.0, math.log(3.0)))
    planted = jax.random.uniform(second_key, (N_REPLICA, HV, 1), jnp.float32) < 1.0 / 32.0
    spikes = jnp.where(planted, 10.0, 1.0)
    noise = jnp.clip(jax.random.normal(prng_partition_part, (N_REPLICA, HV, D), jnp.float32), -5.0, 5.0)
    payload_matrix_lines = base[None] + 0.01 * row_scale * spikes * noise
    return payload_matrix_lines.astype(jnp.float32)


def plant(result, own_key, low, top_value):
    longest = result.shape.index(max(result.shape))
    spots = []
    for shift in (0, 1):
        where = [jax.random.randint(jax.random.fold_in(own_key, axis), (), 0, length) for axis, length in enumerate(result.shape)]
        where[longest] = (where[longest] + shift) % result.shape[longest]
        spots.append(tuple(where))
    return result.at[spots[0]].set(low).at[spots[1]].set(top_value)


def shard_levels(stream_key, extent, cuts, low, top_value):
    factor_of, own = 1.0, jax.random.fold_in(stream_key, 6)
    for dim, parts in cuts:
        draws = jnp.exp(jax.random.uniform(jax.random.fold_in(own, dim), (parts,), jnp.float32, low / len(cuts), top_value / len(cuts)))
        factor_of = factor_of * jnp.repeat(draws, extent[dim] // parts).reshape([-1 if axis == dim else 1 for axis in range(len(extent))])
    return factor_of


def bell_draw(rng, shape, scale, bound, pieces=(), dtype=jnp.bfloat16):
    entries = scale * jax.random.normal(rng, shape, jnp.float32)
    if pieces:
        entries = entries * shard_levels(rng, shape, pieces, -0.22, 0.18)
    return jnp.clip(entries, -bound, bound).astype(dtype)


def setup_inputs(seed: int = 0) -> dict:
    splits = jax.random.split(jax.random.key(seed), 13)
    return {
        "queries": bell_draw(splits[0], (TOKENS, HV), 1.0, 6.0, ((0, 128),)),
        "keys": bell_draw(splits[1], (TOKENS, HV), 1.0, 6.0, ((0, 128),)),
        "values": bell_draw(splits[2], (TOKENS, HV), 1.0, 6.0, ((0, 128),)),
        "log_decay": draw_log_decay(jax.random.fold_in(splits[12], 71), 0),
        "write_strength": jnp.clip(0.1 + 0.9 * jax.random.uniform(splits[4], (OWNED_ATTN_UNITS, TOKENS), jnp.float32) ** shard_levels(splits[4], (OWNED_ATTN_UNITS, TOKENS), ((1, 128),), -0.2, 0.2), 0.1, 1.0),
        "out_grad": bell_draw(splits[5], (TOKENS, D), 1.0, 6.0, ((0, 128),)),
        "replica_weights": draw_replica_weights(jax.random.fold_in(splits[12], 71), 0),
        "adam_first": bell_draw(splits[7], (N_REPLICA, HV, D), 0.1, 1.5, ((0, 8), (1, 16)), jnp.float32),
        "adam_second": jnp.clip(jnp.exp(math.log(0.5) - 2.3025851 * jax.random.uniform(splits[8], (N_REPLICA, HV, D), jnp.float32) ** shard_levels(splits[8], (N_REPLICA, HV, D), ((0, 8), (1, 16)), -0.2, 0.2)), 0.05, 0.5),
        "anchor": draw_anchor(jax.random.fold_in(splits[12], 71), 0),
        "outer_momentum": bell_draw(splits[10], (HV, D), 0.02, 0.3125, ((0, 16),), jnp.float32),
        "exponents": plant(jax.random.randint(splits[11], (N_REPLICA, BLOCKS), -13, -10), jax.random.fold_in(splits[11], 1), -13, (-10) - 1).astype(jnp.int32),
    }


HIGH = lax.Precision.HIGHEST

def delta_core(queries, keys, values, log_decay, write_strength):
    number_of_batches = TOKENS // POSITIONS_PER_GPU
    qf = queries.astype(jnp.float32).reshape(number_of_batches, POSITIONS_PER_GPU, OWNED_ATTN_UNITS, HEAD)
    kf = keys.astype(jnp.float32).reshape(number_of_batches, POSITIONS_PER_GPU, OWNED_ATTN_UNITS, HEAD)
    vf = values.astype(jnp.float32).reshape(number_of_batches, POSITIONS_PER_GPU, OWNED_ATTN_UNITS, HEAD)
    kn = kf / jnp.sqrt(lax.optimization_barrier(jnp.sum(kf * kf, axis=-1, keepdims=True)) + 1e-06)
    qs = qf * HEAD ** (-0.5)
    decay = log_decay.reshape(OWNED_ATTN_UNITS, number_of_batches, POSITIONS_PER_GPU).transpose(1, 2, 0)
    strength = write_strength.reshape(OWNED_ATTN_UNITS, number_of_batches, POSITIONS_PER_GPU).transpose(1, 2, 0)
    inputs = tuple((jnp.swapaxes(item, 0, 1) for item in (qs, kn, vf, decay, strength)))

    def advance(state, item):
        qrow, krow, vrow, grow, brow = item
        aged = jnp.exp(grow)[:, :, None, None] * state
        guess = jnp.einsum('shvk,shk->shv', aged, krow, precision=HIGH)
        state = aged + jnp.einsum('shv,shk->shvk', brow[:, :, None] * (vrow - guess), krow, precision=HIGH)
        return (state, jnp.einsum('shvk,shk->shv', state, qrow, precision=HIGH))
    start = jnp.zeros((number_of_batches, OWNED_ATTN_UNITS, HEAD, HEAD), jnp.float32)
    unused, outputs = lax.scan(advance, start, inputs)
    return jnp.swapaxes(outputs, 0, 1).reshape(TOKENS, HV).astype(jnp.bfloat16)

def reference(queries, keys, values, log_decay, write_strength, out_grad, replica_weights, adam_first, adam_second, anchor, outer_momentum, exponents):
    core = delta_core(queries, keys, values, log_decay, write_strength)
    scale = HV ** (-0.5)
    core_rep = core.reshape(N_REPLICA, N_FSDP, POSITIONS_PER_GPU, HV)
    grad_rep = out_grad.reshape(N_REPLICA, N_FSDP, POSITIONS_PER_GPU, D)

    def one_replica(item):
        core_r, grad_r, weights, first, second, expo = item
        working = weights.astype(jnp.bfloat16)
        rows = core_r.reshape(N_FSDP * POSITIONS_PER_GPU, HV)
        output = (jnp.dot(rows, working, preferred_element_type=jnp.float32) * scale).astype(jnp.bfloat16)

        def add_shard(total, shard):
            part = jnp.dot(shard[0].T, shard[1], preferred_element_type=jnp.float32) * scale
            return (total + part.astype(jnp.bfloat16).astype(jnp.float32), 0)
        grad, unused = lax.scan(add_shard, jnp.zeros((HV, D), jnp.float32), (core_r, grad_r))
        first = 0.9 * first + 0.1 * grad
        second = 0.95 * second + 0.05 * grad * grad
        updated = weights - 0.03 * (first / (jnp.sqrt(second) + 1e-08) + 0.1 * weights)
        delta = anchor - updated
        power = expo.astype(jnp.float32)
        down_scale = jnp.repeat(jnp.exp2(-power), BLOCK)[:, None]
        up_scale = jnp.repeat(jnp.exp2(power), BLOCK)[:, None]
        encoded = jnp.clip(delta * down_scale, -448.0, 448.0).astype(jnp.bfloat16)
        return (output, encoded.astype(jnp.float32) * up_scale)
    outputs, decoded = lax.map(one_replica, (core_rep, grad_rep, replica_weights, adam_first, adam_second, exponents))
    outer_delta = lax.optimization_barrier(jnp.sum(decoded, axis=0)) / N_REPLICA
    new_momentum = 0.9 * outer_momentum + outer_delta
    new_anchor = anchor - 0.7 * (outer_delta + 0.9 * new_momentum)
    return (outputs.reshape(TOKENS, D), new_anchor, new_momentum)
```

```python
import jax
import jax.numpy as jnp
from jax import lax
from jax.experimental import pallas as pl
from jax.experimental.pallas import tpu as pltpu
from jax.sharding import PartitionSpec as P

HEAD = 128
HEADS = 16
SEQ = 256
WIDTH = HEADS * HEAD
D = 4096
BLOCK = 128
REPLICAS = 8
SHARE = BLOCK // REPLICAS
GROUP = 4
GROUPS = HEADS // GROUP
CHUNK = 512
CHUNKS = D // CHUNK
HALF = CHUNK // 2
SIDE = D // 2
SCALE = WIDTH ** (-0.5)
SENDS = 2
F32 = jnp.float32
BF16 = jnp.bfloat16
NT = (((1,), (1,)), ((), ()))
MESH = pl.DeviceIdType.MESH


def split(item):
    high = item.astype(BF16)
    return high, (item - high.astype(F32)).astype(BF16)


def as_left(item):
    return jnp.concatenate(split(item), axis=1)


def as_right(item):
    row = jnp.concatenate(split(item), axis=1)
    return jnp.concatenate((row, row), axis=0)


def product(left, right):
    both = jnp.dot(left, right, preferred_element_type=F32)
    return both[:, :HEAD] + both[:, HEAD:]


def fill_tables(keys, log_decay, strength, rows, cols):
    i = lax.broadcasted_iota(jnp.int32, (SEQ, SEQ), 0)
    j = lax.broadcasted_iota(jnp.int32, (SEQ, SEQ), 1)
    upto = jnp.where(i <= j, 1.0, 0.0).astype(F32)
    sums = jnp.dot(
        log_decay[...], upto, preferred_element_type=F32, precision=lax.Precision.HIGHEST
    )
    ones = jnp.ones((8, HEAD), BF16)
    rows[...] = jnp.zeros_like(rows)
    for g in range(GROUPS):
        rows[g, 0:GROUP, :] = sums[g * GROUP : (g + 1) * GROUP]
        rows[g, GROUP : 2 * GROUP, :] = strength[g * GROUP : (g + 1) * GROUP, :]
        for n in range(GROUP):
            h = g * GROUP + n
            key = keys[:, h * HEAD : (h + 1) * HEAD].astype(F32)
            high, low = split(key * key)
            total = lax.dot_general(ones, high, NT, preferred_element_type=F32)
            total = total + lax.dot_general(ones, low, NT, preferred_element_type=F32)
            rows[g, 2 * GROUP + n : 2 * GROUP + n + 1, :] = lax.rsqrt(total[0:1] + 1e-6)
        cols[g] = rows[g].T


def delta_group(g, queries, keys, values, rows, cols):
    i = lax.broadcasted_iota(jnp.int32, (HEAD, HEAD), 0)
    j = lax.broadcasted_iota(jnp.int32, (HEAD, HEAD), 1)
    col = cols[g]
    low, strict = i >= j, i > j
    couple_1, couple_2, cross, mix_1, mix_2, mix_cross, sides = [], [], [], [], [], [], []
    for n in range(GROUP):
        at = pl.ds(pl.multiple_of((g * GROUP + n) * HEAD, HEAD), HEAD)
        query, key = queries[:, at], keys[:, at]
        decay_row = rows[g, n : n + 1, :]
        norm_row = rows[g, 2 * GROUP + n : 2 * GROUP + n + 1, :]
        decay_col = col[:, n : n + 1]
        strength = col[:, GROUP + n : GROUP + n + 1]
        scaled = strength * col[:, 2 * GROUP + n : 2 * GROUP + n + 1]
        dots = lax.dot_general(
            jnp.concatenate((key, query), axis=0), key, NT, preferred_element_type=F32
        )
        left_norm, right_norm = norm_row[:, :HEAD], norm_row[:, HEAD:]
        gap_1 = decay_col[:HEAD] - decay_row[:, :HEAD]
        gap_2 = decay_col[HEAD:] - decay_row[:, HEAD:]
        gap_cross = decay_col[HEAD:] - decay_row[:, :HEAD]
        fade_1 = jnp.exp(jnp.where(low, gap_1, -1e30)) * left_norm
        fade_2 = jnp.exp(jnp.where(low, gap_2, -1e30)) * right_norm
        fade_cross = jnp.exp(jnp.minimum(gap_cross, 0.0)) * left_norm
        couple_1.append(jnp.where(strict, dots[:HEAD, :HEAD] * fade_1 * scaled[:HEAD], 0.0))
        couple_2.append(jnp.where(strict, dots[HEAD:SEQ, HEAD:] * fade_2 * scaled[HEAD:], 0.0))
        cross.append(dots[HEAD:SEQ, :HEAD] * fade_cross * scaled[HEAD:])
        size = HEAD ** (-0.5)
        mix_1.append(dots[SEQ : SEQ + HEAD, :HEAD] * fade_1 * size)
        mix_2.append(dots[SEQ + HEAD :, HEAD:] * fade_2 * size)
        mix_cross.append(dots[SEQ + HEAD :, :HEAD] * fade_cross * size)
        sides.append(strength * values[:, at].astype(F32))
    couples = couple_1 + couple_2
    eye = jnp.where(i == j, 1.0, 0.0).astype(F32)
    inverse = [eye - jnp.where(i // 2 == j // 2, couple, 0.0) for couple in couples]
    size = 2
    while size < HEAD:
        below = (i // (2 * size) == j // (2 * size)) & (i % (2 * size) >= size) & (j % (2 * size) < size)
        lefts = [as_left(jnp.where(below, couple, 0.0)) for couple in couples]
        steps = [product(left, as_right(item)) for left, item in zip(lefts, inverse)]
        inverse = [item - product(as_left(item), as_right(step)) for item, step in zip(inverse, steps)]
        size *= 2
    results = []
    fresh_1 = [product(as_left(inverse[n]), as_right(sides[n][:HEAD])) for n in range(GROUP)]
    uses = [
        product(
            as_left(jnp.concatenate((cross[n], mix_1[n], mix_cross[n]), axis=0)), as_right(fresh_1[n])
        )
        for n in range(GROUP)
    ]
    fresh_2 = [
        product(as_left(inverse[GROUP + n]), as_right(sides[n][HEAD:] - uses[n][:HEAD]))
        for n in range(GROUP)
    ]
    for n in range(GROUP):
        second = uses[n][2 * HEAD :] + product(as_left(mix_2[n]), as_right(fresh_2[n]))
        results.append(jnp.concatenate((uses[n][HEAD : 2 * HEAD], second), axis=0))
    return results


def kernel(
    queries_hbm, keys_hbm, values_hbm, decay_hbm, strength_hbm, out_grad_hbm, weights_hbm,
    first_hbm, second_hbm, anchor_hbm, momentum_hbm, exponents,
    layer_out_hbm, new_anchor_hbm, new_momentum_hbm,
    queries, keys, values, decay, strength, weights, first, second, anchor, momentum,
    rows, cols, core, core_t, core_quad, grad_quad, every_weight, partial,
    relay_up, relay_down, sum_up, sum_down, decoded, shares, outer,
    load_sem, store_sem, grad_send, grad_recv, core_send, core_recv, row_send, row_recv,
    pair_send, pair_recv, relay_send, relay_recv, sum_send, sum_recv,
    share_send, share_recv, outer_send, outer_recv,
):
    replica, me = lax.axis_index("replica"), lax.axis_index("fsdp")
    x, y, c = me // 8, (me // 2) % 4, me % 2

    def index(x_at, y_at, c_at):
        return x_at * 8 + lax.rem(y_at + 4, 4) * 2 + c_at

    def device(f):
        return {"replica": replica, "fsdp": f}

    sibling, across, corner = index(x, y, 1 - c), index(1 - x, y, c), index(1 - x, y, 1 - c)
    up, down = index(x, y + 1, c), index(x, y - 1, c)
    others = [lax.rem(replica + k, REPLICAS) for k in range(1, REPLICAS)]
    member = x * 2 + c
    member_sibling, member_across, member_corner = x * 2 + 1 - c, (1 - x) * 2 + c, (1 - x) * 2 + 1 - c

    started = []

    def copy(src, dst, send_sem, recv_sem, to):
        return pltpu.make_async_remote_copy(
            src_ref=src, dst_ref=dst, send_sem=send_sem, recv_sem=recv_sem,
            device_id=to, device_id_type=MESH,
        )

    def send(src, dst, send_sem, recv_sem, to):
        item = copy(src, dst, send_sem, recv_sem, to)
        item.start()
        started.append(item)

    def arrived(region, recv_sem):
        copy(region, region, recv_sem, recv_sem, device(sibling)).wait_recv()

    grad_own = grad_quad.at[pl.ds(pl.multiple_of(member * SEQ, SEQ), SEQ)]
    loads = [
        (weights_hbm.at[0], weights), (keys_hbm, keys), (decay_hbm, decay), (strength_hbm, strength),
        (queries_hbm, queries), (values_hbm, values), (out_grad_hbm, grad_own), (first_hbm.at[0], first),
        (second_hbm.at[0], second), (anchor_hbm, anchor), (momentum_hbm, momentum),
    ]
    loads = [pltpu.make_async_copy(src, dst, load_sem.at[n]) for n, (src, dst) in enumerate(loads)]
    for load in loads:
        load.start()

    barrier = pltpu.get_barrier_semaphore()
    peers = [device(f) for f in (sibling, across, corner, up, down)]
    peers += [{"replica": r, "fsdp": me} for r in others]
    for peer in peers:
        pl.semaphore_signal(barrier, inc=1, device_id=peer, device_id_type=MESH)
    pl.semaphore_wait(barrier, len(peers))

    def grad_part(who, j):
        return grad_quad.at[
            pl.ds(pl.multiple_of(who * SEQ, SEQ), SEQ), pl.ds(j * CHUNK, CHUNK)
        ]

    def send_grad(j):
        src = out_grad_hbm.at[:, pl.ds(j * CHUNK, CHUNK)]
        send(src, grad_part(member, j), grad_send.at[0, j], grad_recv.at[0, j], device(across))
        send(src, grad_part(member, j), grad_send.at[1, j], grad_recv.at[1, j], device(sibling))

    def pass_grad(j):
        arrived(grad_part(member_across, j), grad_recv.at[0, j])
        send(
            grad_part(member_across, j), grad_part(member_across, j),
            grad_send.at[2, j], grad_recv.at[2, j], device(sibling),
        )

    def weight_rows(f):
        return every_weight.at[pl.ds(pl.multiple_of(f * BLOCK, BLOCK), BLOCK)]

    def weight_side(f, side):
        return every_weight.at[
            pl.ds(pl.multiple_of(f * BLOCK, BLOCK), BLOCK), pl.ds(side * SIDE, SIDE)
        ]

    def ring(u, k, f, side, to):
        send(weight_side(f, side), weight_side(f, side), row_send.at[u, k], row_recv.at[u, k], device(to))

    def share_weight(u, k, f):
        send(weight_rows(f), weight_rows(f), pair_send.at[u, k], pair_recv.at[u, k], device(sibling))

    column = (x, 1 - x)

    def ring_first(u):
        block = index(column[u], y, c)
        ring(u, 0, block, 0, up)
        ring(u, 1, block, 1, down)
        ring(u, 2, block, 1, up)
        ring(u, 3, block, 0, down)
        share_weight(u, 0, block)

    def ring_second(u):
        below, above = index(column[u], y - 1, c), index(column[u], y + 1, c)
        arrived(weight_side(below, 0), row_recv.at[u, 0])
        ring(u, 4, below, 0, up)
        arrived(weight_side(above, 1), row_recv.at[u, 1])
        ring(u, 5, above, 1, down)

    def share_near(u):
        below, above = index(column[u], y - 1, c), index(column[u], y + 1, c)
        arrived(weight_side(below, 1), row_recv.at[u, 2])
        share_weight(u, 1, below)
        arrived(weight_side(above, 0), row_recv.at[u, 3])
        share_weight(u, 2, above)

    def share_far(u):
        far = index(column[u], y + 2, c)
        arrived(weight_side(far, 0), row_recv.at[u, 4])
        arrived(weight_side(far, 1), row_recv.at[u, 5])
        share_weight(u, 3, far)

    def from_sibling(u, k):
        shift = (0, -1, 1, 2)[k]
        arrived(weight_rows(index(column[u], y + shift, 1 - c)), pair_recv.at[u, k])

    for j in range(2):
        send_grad(j)
    loads[0].wait()
    weight_rows(me)[...] = weights[...].astype(BF16)
    ring_first(0)
    send(weight_rows(me), weight_rows(me), pair_send.at[0, 4], pair_recv.at[0, 4], device(across))
    for j in range(2, CHUNKS):
        send_grad(j)

    for n in range(1, 6):
        loads[n].wait()
    fill_tables(keys, decay, strength, rows, cols)

    def quad_part(who, y_at):
        return core_quad.at[
            pl.ds(pl.multiple_of(y_at * HEAD, HEAD), HEAD), pl.ds(pl.multiple_of(who * SEQ, SEQ), SEQ)
        ]

    def head_copy(g, n):
        h = g * GROUP + n
        x_at, y_at, c_at = g // 2, (g % 2) * 2 + n // 2, n % 2
        mine = (x_at == x) & (c_at == c)
        item = copy(
            core_t.at[pl.ds(pl.multiple_of(h * HEAD, HEAD), HEAD)], quad_part(member, y_at),
            core_send.at[h], core_recv.at[member, y_at], device(index(x_at, y, c_at)),
        )
        return mine, y_at, item

    def heads(g, carry):
        results = delta_group(g, queries, keys, values, rows, cols)
        for n, result in enumerate(results):
            at = pl.ds(pl.multiple_of((g * GROUP + n) * HEAD, HEAD), HEAD)
            core[:, at] = result.astype(BF16)
            turned = result.T.astype(BF16)
            core_t[at, :] = turned
            mine, y_at, item = head_copy(g, n)

            @pl.when(mine)
            def _():
                quad_part(member, y_at)[...] = turned

            @pl.when(jnp.logical_not(mine))
            def _():
                item.start()

        return carry

    lax.fori_loop(0, GROUPS, heads, 0)

    def partial_at(shift, start, size):
        return partial.at[
            pl.ds(pl.multiple_of(lax.rem(y + shift + 4, 4) * BLOCK, BLOCK), BLOCK), pl.ds(start, size)
        ]

    def take_grad(j):
        arrived(grad_part(member_sibling, j), grad_recv.at[1, j])
        arrived(grad_part(member_corner, j), grad_recv.at[2, j])

    def partial_chunk(j):
        at = pl.ds(j * CHUNK, CHUNK)
        total = jnp.dot(core_quad[...], grad_quad[:, at], preferred_element_type=F32)
        partial[:, at] = (total * SCALE).astype(BF16)
        start, half = j * CHUNK, pl.ds(j * HALF, HALF)
        send(
            partial_at(2, start, HALF), relay_up.at[:, half],
            relay_send.at[0, j], relay_recv.at[0, j], device(up),
        )
        send(
            partial_at(2, start + HALF, HALF), relay_down.at[:, half],
            relay_send.at[1, j], relay_recv.at[1, j], device(down),
        )

    def relay_chunk(j):
        start, at, half = j * CHUNK, pl.ds(j * CHUNK, CHUNK), pl.ds(j * HALF, HALF)
        for shift, relay, k, place in ((1, relay_up, 0, start), (-1, relay_down, 1, start + HALF)):
            arrived(relay.at[:, half], relay_recv.at[k, j])
            spot = partial_at(shift, place, HALF)
            spot[...] = (spot[...].astype(F32) + relay[:, half].astype(F32)).astype(BF16)
        send(partial_at(1, start, CHUNK), sum_up.at[:, at], sum_send.at[0, j], sum_recv.at[0, j], device(up))
        send(partial_at(-1, start, CHUNK), sum_down.at[:, at], sum_send.at[1, j], sum_recv.at[1, j], device(down))

    power = jnp.full((1, 128), exponents[0, 0], jnp.int32).astype(F32)
    down_scale, up_scale = jnp.exp2(-power)[:, :1], jnp.exp2(power)[:, :1]

    def update_chunk(j):
        at = pl.ds(j * CHUNK, CHUNK)
        arrived(sum_up.at[:, at], sum_recv.at[0, j])
        arrived(sum_down.at[:, at], sum_recv.at[1, j])
        grad = partial_at(0, j * CHUNK, CHUNK)[...].astype(F32)
        grad = grad + sum_up[:, at].astype(F32) + sum_down[:, at].astype(F32)
        weight, base = weights[:, at], anchor[:, at]
        one = 0.9 * first[:, at] + 0.1 * grad
        two = 0.95 * second[:, at] + 0.05 * grad * grad
        updated = weight - 0.03 * (one / (jnp.sqrt(two) + 1e-08) + 0.1 * weight)
        encoded = jnp.clip((base - updated) * down_scale, -448.0, 448.0).astype(BF16)
        decoded[:, at] = (encoded.astype(F32) * up_scale).astype(BF16)
        if j % SENDS == SENDS - 1:
            group = j // SENDS
            span = pl.ds(group * SENDS * CHUNK, SENDS * CHUNK)
            for k, r in enumerate(others):
                send(
                    decoded.at[pl.ds(pl.multiple_of(r * SHARE, SHARE), SHARE), span],
                    shares.at[replica, :, span],
                    share_send.at[k, group], share_recv.at[replica, group],
                    {"replica": r, "fsdp": me},
                )

    for n in range(6, 11):
        loads[n].wait()
    ring_second(0)
    for yy in range(4):
        for who in (member_sibling, member_across, member_corner):
            arrived(quad_part(who, yy), core_recv.at[who, yy])

    for j in range(CHUNKS):
        pass_grad(j)
        if j >= 2:
            update_chunk(j - 2)
        if j >= 1:
            relay_chunk(j - 1)
        take_grad(j)
        partial_chunk(j)
        if j == 1:
            arrived(weight_rows(across), pair_recv.at[0, 4])
            ring_first(1)
        if j == 2:
            share_near(0)
        if j == 3:
            share_far(0)
    relay_chunk(CHUNKS - 1)
    update_chunk(CHUNKS - 2)
    ring_second(1)
    update_chunk(CHUNKS - 1)

    def outer_rows(r):
        return outer.at[pl.ds(pl.multiple_of(r * SHARE, SHARE), SHARE)]

    for group in range(CHUNKS // SENDS):
        span = pl.ds(group * SENDS * CHUNK, SENDS * CHUNK)
        for r in others:
            arrived(shares.at[r, :, span], share_recv.at[r, group])
    shares[replica] = decoded[pl.ds(pl.multiple_of(replica * SHARE, SHARE), SHARE), :]
    total = shares[0].astype(F32)
    for r in range(1, REPLICAS):
        total = total + shares[r].astype(F32)
    outer_rows(replica)[...] = (total * (1.0 / REPLICAS)).astype(BF16)
    for k, r in enumerate(others):
        send(
            outer_rows(replica), outer_rows(replica), outer_send.at[k], outer_recv.at[replica],
            {"replica": r, "fsdp": me},
        )

    def rows_of(x_at, y_at):
        return pl.multiple_of(x_at * 1024 + lax.rem(y_at + 4, 4) * 256, 256)

    def multiply(spots, size, begin, finish):
        def tile(n, carry):
            at = pl.ds(pl.multiple_of(n * CHUNK, CHUNK), CHUNK)
            total = None
            for spot in spots:
                term = jnp.dot(
                    core[:, pl.ds(spot, size)], every_weight[pl.ds(spot, size), at],
                    preferred_element_type=F32,
                )
                total = term if total is None else total + term
            if not begin:
                total = total + jnp.concatenate((first[:, at], second[:, at]), axis=0)
            if finish:
                partial[0:SEQ, at] = (total * SCALE).astype(BF16)
            else:
                first[:, at] = total[:BLOCK]
                second[:, at] = total[BLOCK:]
            return carry

        lax.fori_loop(0, CHUNKS, tile, 0)

    for k in range(4):
        from_sibling(0, k)
    multiply([pl.multiple_of(x * 1024, 1024)], 1024, True, False)
    share_near(1)

    def outer_step(r):
        spot = pl.ds(pl.multiple_of(r * SHARE, SHARE), SHARE)
        delta = outer[spot, :].astype(F32)
        moved = 0.9 * momentum[spot, :] + delta
        momentum[spot, :] = moved
        anchor[spot, :] = anchor[spot, :] - 0.7 * (delta + 0.9 * moved)

    outer_step(replica)
    for r in others:
        arrived(outer_rows(r), outer_recv.at[r])
        outer_step(r)
    stores = [
        pltpu.make_async_copy(anchor, new_anchor_hbm, store_sem.at[0]),
        pltpu.make_async_copy(momentum, new_momentum_hbm, store_sem.at[1]),
    ]
    for store in stores:
        store.start()

    for k in range(3):
        from_sibling(1, k)
    multiply([rows_of(1 - x, y + shift) for shift in (0, -1, 1)], 256, False, False)
    share_far(1)
    from_sibling(1, 3)
    for item in started:
        item.wait_send()
    multiply([rows_of(1 - x, y + 2)], 256, False, True)
    last = pltpu.make_async_copy(partial.at[0:SEQ], layer_out_hbm, store_sem.at[2])
    last.start()

    def finish_heads(g, carry):
        for n in range(GROUP):
            mine, _, item = head_copy(g, n)

            @pl.when(jnp.logical_not(mine))
            def _():
                item.wait_send()

        return carry

    lax.fori_loop(0, GROUPS, finish_heads, 0)
    for store in stores:
        store.wait()
    last.wait()


def on_device(
    queries, keys, values, log_decay, write_strength, out_grad, replica_weights,
    adam_first, adam_second, anchor, outer_momentum, exponents,
):
    dma = pltpu.SemaphoreType.DMA
    scratch = [
        pltpu.VMEM((SEQ, WIDTH), BF16),
        pltpu.VMEM((SEQ, WIDTH), BF16),
        pltpu.VMEM((SEQ, WIDTH), BF16),
        pltpu.VMEM((HEADS, SEQ), F32),
        pltpu.VMEM((HEADS, SEQ), F32),
        pltpu.VMEM((BLOCK, D), F32),
        pltpu.VMEM((BLOCK, D), F32),
        pltpu.VMEM((BLOCK, D), F32),
        pltpu.VMEM((BLOCK, D), F32),
        pltpu.VMEM((BLOCK, D), F32),
        pltpu.VMEM((GROUPS, 128, SEQ), F32),
        pltpu.VMEM((GROUPS, SEQ, 128), F32),
        pltpu.VMEM((SEQ, WIDTH), BF16),
        pltpu.VMEM((WIDTH, SEQ), BF16),
        pltpu.VMEM((4 * HEAD, 4 * SEQ), BF16),
        pltpu.VMEM((4 * SEQ, D), BF16),
        pltpu.VMEM((WIDTH, D), BF16),
        pltpu.VMEM((4 * BLOCK, D), BF16),
        pltpu.VMEM((BLOCK, SIDE), BF16),
        pltpu.VMEM((BLOCK, SIDE), BF16),
        pltpu.VMEM((BLOCK, D), BF16),
        pltpu.VMEM((BLOCK, D), BF16),
        pltpu.VMEM((BLOCK, D), BF16),
        pltpu.VMEM((REPLICAS, SHARE, D), BF16),
        pltpu.VMEM((BLOCK, D), BF16),
        dma((11,)), dma((3,)),
        dma((3, CHUNKS)), dma((3, CHUNKS)),
        dma((HEADS,)), dma((4, 4)),
        dma((2, 6)), dma((2, 6)),
        dma((2, 5)), dma((2, 5)),
        dma((2, CHUNKS)), dma((2, CHUNKS)),
        dma((2, CHUNKS)), dma((2, CHUNKS)),
        dma((REPLICAS - 1, CHUNKS // SENDS)), dma((REPLICAS, CHUNKS // SENDS)),
        dma((REPLICAS - 1,)), dma((REPLICAS,)),
    ]
    anywhere = pl.BlockSpec(memory_space=pl.ANY)
    return pl.pallas_call(
        kernel,
        out_shape=(
            jax.ShapeDtypeStruct((SEQ, D), BF16),
            jax.ShapeDtypeStruct((BLOCK, D), F32),
            jax.ShapeDtypeStruct((BLOCK, D), F32),
        ),
        in_specs=[anywhere] * 11 + [pl.BlockSpec(memory_space=pltpu.SMEM)],
        out_specs=(anywhere,) * 3,
        scratch_shapes=scratch,
        compiler_params=pltpu.CompilerParams(
            collective_id=0, has_side_effects=True, vmem_limit_bytes=60 * 1024 * 1024
        ),
        name="diloco_step",
    )(
        queries, keys, values, log_decay, write_strength, out_grad, replica_weights,
        adam_first, adam_second, anchor, outer_momentum, exponents,
    )


def solution(mesh):
    return jax.shard_map(
        on_device,
        mesh=mesh,
        in_specs=(
            P(("replica", "fsdp"), None),
            P(("replica", "fsdp"), None),
            P(("replica", "fsdp"), None),
            P(None, ("replica", "fsdp")),
            P(None, ("replica", "fsdp")),
            P(("replica", "fsdp"), None),
            P("replica", "fsdp", None),
            P("replica", "fsdp", None),
            P("replica", "fsdp", None),
            P("fsdp", None),
            P("fsdp", None),
            P("replica", "fsdp"),
        ),
        out_specs=(P(("replica", "fsdp"), None), P("fsdp", None), P("fsdp", None)),
        check_vma=False,
    )
```

```python
import jax
import jax.numpy as jnp
from jax import lax
from jax.experimental import pallas as pl
from jax.experimental.pallas import tpu as pltpu
from jax.sharding import PartitionSpec as P

HEAD = 128
HEADS = 16
SEQ = 256
WIDTH = HEADS * HEAD
D = 4096
BLOCK = 128
REPLICAS = 8
SHARE = BLOCK // 4
GROUP = 4
GROUPS = HEADS // GROUP
CHUNK = 512
CHUNKS = D // CHUNK
HALF = CHUNK // 2
SIDE = D // 2
QUARTER = D // 4
EARLY = 2
SCALE = WIDTH ** (-0.5)
SENDS = 2
SPAN = SENDS * CHUNK
F32 = jnp.float32
BF16 = jnp.bfloat16
NT = (((1,), (1,)), ((), ()))
MESH = pl.DeviceIdType.MESH


def split(item):
    high = item.astype(BF16)
    return high, (item - high.astype(F32)).astype(BF16)


def as_left(item):
    return jnp.concatenate(split(item), axis=1)


def as_right(item):
    row = jnp.concatenate(split(item), axis=1)
    return jnp.concatenate((row, row), axis=0)


def product(left, right):
    both = jnp.dot(left, right, preferred_element_type=F32)
    return both[:, :HEAD] + both[:, HEAD:]


def fill_tables(keys, log_decay, strength, rows, cols):
    i = lax.broadcasted_iota(jnp.int32, (SEQ, SEQ), 0)
    j = lax.broadcasted_iota(jnp.int32, (SEQ, SEQ), 1)
    upto = jnp.where(i <= j, 1.0, 0.0).astype(F32)
    sums = jnp.dot(
        log_decay[...], upto, preferred_element_type=F32, precision=lax.Precision.HIGHEST
    )
    ones = jnp.ones((8, HEAD), BF16)
    rows[...] = jnp.zeros_like(rows)
    for g in range(GROUPS):
        rows[g, 0:GROUP, :] = sums[g * GROUP : (g + 1) * GROUP]
        rows[g, GROUP : 2 * GROUP, :] = strength[g * GROUP : (g + 1) * GROUP, :]
        for n in range(GROUP):
            h = g * GROUP + n
            key = keys[:, h * HEAD : (h + 1) * HEAD].astype(F32)
            high, low = split(key * key)
            total = lax.dot_general(ones, high, NT, preferred_element_type=F32)
            total = total + lax.dot_general(ones, low, NT, preferred_element_type=F32)
            rows[g, 2 * GROUP + n : 2 * GROUP + n + 1, :] = lax.rsqrt(total[0:1] + 1e-6)
        cols[g] = rows[g].T


def delta_group(g, queries, keys, values, rows, cols):
    i = lax.broadcasted_iota(jnp.int32, (HEAD, HEAD), 0)
    j = lax.broadcasted_iota(jnp.int32, (HEAD, HEAD), 1)
    col = cols[g]
    low, strict = i >= j, i > j
    couple_1, couple_2, cross, mix_1, mix_2, mix_cross, sides = [], [], [], [], [], [], []
    for n in range(GROUP):
        at = pl.ds(pl.multiple_of((g * GROUP + n) * HEAD, HEAD), HEAD)
        query, key = queries[:, at], keys[:, at]
        decay_row = rows[g, n : n + 1, :]
        norm_row = rows[g, 2 * GROUP + n : 2 * GROUP + n + 1, :]
        decay_col = col[:, n : n + 1]
        strength = col[:, GROUP + n : GROUP + n + 1]
        scaled = strength * col[:, 2 * GROUP + n : 2 * GROUP + n + 1]
        dots = lax.dot_general(
            jnp.concatenate((key, query), axis=0), key, NT, preferred_element_type=F32
        )
        left_norm, right_norm = norm_row[:, :HEAD], norm_row[:, HEAD:]
        gap_1 = decay_col[:HEAD] - decay_row[:, :HEAD]
        gap_2 = decay_col[HEAD:] - decay_row[:, HEAD:]
        gap_cross = decay_col[HEAD:] - decay_row[:, :HEAD]
        fade_1 = jnp.exp(jnp.where(low, gap_1, -1e30)) * left_norm
        fade_2 = jnp.exp(jnp.where(low, gap_2, -1e30)) * right_norm
        fade_cross = jnp.exp(jnp.minimum(gap_cross, 0.0)) * left_norm
        couple_1.append(jnp.where(strict, dots[:HEAD, :HEAD] * fade_1 * scaled[:HEAD], 0.0))
        couple_2.append(jnp.where(strict, dots[HEAD:SEQ, HEAD:] * fade_2 * scaled[HEAD:], 0.0))
        cross.append(dots[HEAD:SEQ, :HEAD] * fade_cross * scaled[HEAD:])
        size = HEAD ** (-0.5)
        mix_1.append(dots[SEQ : SEQ + HEAD, :HEAD] * fade_1 * size)
        mix_2.append(dots[SEQ + HEAD :, HEAD:] * fade_2 * size)
        mix_cross.append(dots[SEQ + HEAD :, :HEAD] * fade_cross * size)
        sides.append(strength * values[:, at].astype(F32))
    couples = couple_1 + couple_2
    eye = jnp.where(i == j, 1.0, 0.0).astype(F32)
    inverse = [eye - jnp.where(i // 2 == j // 2, couple, 0.0) for couple in couples]
    size = 2
    while size < HEAD:
        below = (i // (2 * size) == j // (2 * size)) & (i % (2 * size) >= size) & (j % (2 * size) < size)
        lefts = [as_left(jnp.where(below, couple, 0.0)) for couple in couples]
        steps = [product(left, as_right(item)) for left, item in zip(lefts, inverse)]
        inverse = [item - product(as_left(item), as_right(step)) for item, step in zip(inverse, steps)]
        size *= 2
    results = []
    fresh_1 = [product(as_left(inverse[n]), as_right(sides[n][:HEAD])) for n in range(GROUP)]
    uses = [
        product(
            as_left(jnp.concatenate((cross[n], mix_1[n], mix_cross[n]), axis=0)), as_right(fresh_1[n])
        )
        for n in range(GROUP)
    ]
    fresh_2 = [
        product(as_left(inverse[GROUP + n]), as_right(sides[n][HEAD:] - uses[n][:HEAD]))
        for n in range(GROUP)
    ]
    for n in range(GROUP):
        second = uses[n][2 * HEAD :] + product(as_left(mix_2[n]), as_right(fresh_2[n]))
        results.append(jnp.concatenate((uses[n][HEAD : 2 * HEAD], second), axis=0))
    return results


def kernel(
    queries_hbm, keys_hbm, values_hbm, decay_hbm, strength_hbm, out_grad_hbm, weights_hbm,
    first_hbm, second_hbm, anchor_hbm, momentum_hbm, exponents,
    layer_out_hbm, new_anchor_hbm, new_momentum_hbm,
    queries, keys, values, decay, strength, weights, first, second, anchor, momentum,
    rows, cols, core, core_t, across_t, across_n, out_sent, out_across, core_quad, grad_quad, every_weight, partial,
    relay_up, relay_down, sum_up, sum_down, decoded, shares, halves, outer,
    load_sem, store_sem, grad_send, grad_recv, quad_send, quad_recv, row_send, row_recv,
    pair_send, pair_recv, cross_send, cross_recv, out_send, out_recv, relay_send, relay_recv, sum_send, sum_recv,
    share_send, share_recv, half_send, half_recv, outer_send, outer_recv,
):
    replica, me = lax.axis_index("replica"), lax.axis_index("fsdp")
    x, y, c = me // 8, (me // 2) % 4, me % 2

    def index(x_at, y_at, c_at):
        return x_at * 8 + lax.rem(y_at + 4, 4) * 2 + c_at

    def device(f):
        return {"replica": replica, "fsdp": f}

    sibling, across, corner = index(x, y, 1 - c), index(1 - x, y, c), index(1 - x, y, 1 - c)
    up, down = index(x, y + 1, c), index(x, y - 1, c)
    z = lax.rem(replica, 4)
    half = replica // 4
    others = [lax.rem(z + k, 4) for k in range(1, 4)]

    def replica_at(half_at, z_at):
        return {"replica": half_at * 4 + z_at, "fsdp": me}

    member = x * 2 + c
    member_sibling, member_across, member_corner = x * 2 + 1 - c, (1 - x) * 2 + c, (1 - x) * 2 + 1 - c

    started, late = [], []

    def copy(src, dst, send_sem, recv_sem, to):
        return pltpu.make_async_remote_copy(
            src_ref=src, dst_ref=dst, send_sem=send_sem, recv_sem=recv_sem,
            device_id=to, device_id_type=MESH,
        )

    def send(src, dst, send_sem, recv_sem, to, kept=started):
        item = copy(src, dst, send_sem, recv_sem, to)
        item.start()
        kept.append(item)

    def arrived(region, recv_sem):
        copy(region, region, recv_sem, recv_sem, device(sibling)).wait_recv()

    grad_own = grad_quad.at[pl.ds(pl.multiple_of(member * SEQ, SEQ), SEQ)]
    loads = [
        (weights_hbm.at[0], weights), (keys_hbm, keys), (decay_hbm, decay), (strength_hbm, strength),
        (queries_hbm, queries), (values_hbm, values), (out_grad_hbm, grad_own), (first_hbm.at[0], first),
        (second_hbm.at[0], second), (anchor_hbm, anchor), (momentum_hbm, momentum),
    ]
    loads = [pltpu.make_async_copy(src, dst, load_sem.at[n]) for n, (src, dst) in enumerate(loads)]
    for load in loads[:6]:
        load.start()

    barrier = pltpu.get_barrier_semaphore()
    peers = [device(f) for f in (sibling, across, corner, up, down)]
    peers += [replica_at(half, zz) for zz in others] + [replica_at(1 - half, z)]
    for peer in peers:
        pl.semaphore_signal(barrier, inc=1, device_id=peer, device_id_type=MESH)
    pl.semaphore_wait(barrier, len(peers))

    def weight_rows(f):
        return every_weight.at[pl.ds(pl.multiple_of(f * BLOCK, BLOCK), BLOCK)]

    def grad_part(who, j):
        return grad_quad.at[
            pl.ds(pl.multiple_of(who * SEQ, SEQ), SEQ), pl.ds(j * CHUNK, CHUNK)
        ]

    def send_grad(j):
        src = out_grad_hbm.at[:, pl.ds(j * CHUNK, CHUNK)]
        send(src, grad_part(member, j), grad_send.at[0, j], grad_recv.at[0, j], device(across))
        send(src, grad_part(member, j), grad_send.at[1, j], grad_recv.at[1, j], device(sibling))

    def pass_grad(j):
        arrived(grad_part(member_across, j), grad_recv.at[0, j])
        send(
            grad_part(member_across, j), grad_part(member_across, j),
            grad_send.at[2, j], grad_recv.at[2, j], device(sibling),
        )

    def weight_part(f, start, size):
        return every_weight.at[
            pl.ds(pl.multiple_of(f * BLOCK, BLOCK), BLOCK), pl.ds(start, size)
        ]

    def weight_side(f, side):
        return weight_part(f, side * SIDE, SIDE)

    def ring(u, side, k, f, half, to):
        part = weight_part(f, side * SIDE + half * QUARTER, QUARTER)
        send(part, part, row_send.at[u, side, k], row_recv.at[u, side, k], device(to), (started, late)[u])

    def ring_arrived(u, side, k, f, half):
        arrived(weight_part(f, side * SIDE + half * QUARTER, QUARTER), row_recv.at[u, side, k])

    def share_weight(u, side, k, f):
        part = weight_side(f, side)
        send(
            part, part, pair_send.at[u, side, k], pair_recv.at[u, side, k], device(sibling), (started, late)[u]
        )

    column = (x, 1 - x)

    def ring_first(u, side, step):
        block = index(column[u], y, c)
        ring(u, side, 2 * step, block, step, up)
        ring(u, side, 2 * step + 1, block, 1 - step, down)

    def ring_second(u, side):
        below, above = index(column[u], y - 1, c), index(column[u], y + 1, c)
        ring_arrived(u, side, 0, below, 0)
        ring(u, side, 4, below, 0, up)
        ring_arrived(u, side, 1, above, 1)
        ring(u, side, 5, above, 1, down)

    def share_near(u, side):
        below, above = index(column[u], y - 1, c), index(column[u], y + 1, c)
        ring_arrived(u, side, 2, below, 1)
        share_weight(u, side, 1, below)
        ring_arrived(u, side, 3, above, 0)
        share_weight(u, side, 2, above)

    def share_far(u, side):
        far = index(column[u], y + 2, c)
        ring_arrived(u, side, 4, far, 0)
        ring_arrived(u, side, 5, far, 1)
        share_weight(u, side, 3, far)

    def from_sibling(u, side, k):
        shift = (0, -1, 1, 2)[k]
        arrived(weight_side(index(column[u], y + shift, 1 - c), side), pair_recv.at[u, side, k])

    for j in range(EARLY):
        send_grad(j)
    loads[0].wait()
    weight_rows(me)[...] = weights[...].astype(BF16)
    for side in range(2):
        ring_first(0, side, 0)
        ring_first(0, side, 1)
    for side in range(2):
        share_weight(0, side, 0, me)
    for load in loads[6:]:
        load.start()

    for n in range(1, 6):
        loads[n].wait()
    fill_tables(keys, decay, strength, rows, cols)

    def heads(g, carry):
        results = delta_group(g, queries, keys, values, rows, cols)
        for n, result in enumerate(results):
            at = pl.ds(pl.multiple_of((g * GROUP + n) * HEAD, HEAD), HEAD)
            core[:, at] = result.astype(BF16)
            core_t[at, :] = result.T.astype(BF16)
        return carry

    lax.fori_loop((1 - x) * 2, (1 - x) * 2 + 2, heads, 0)
    ring_second(0, 0)
    other_rows = core_t.at[pl.ds(pl.multiple_of((1 - x) * 1024, 1024), 1024)]
    send(other_rows, across_t, cross_send.at[0], cross_recv.at[0], device(across))
    for j in range(EARLY, CHUNKS):
        send_grad(j)
    part = weight_side(me, 0)
    send(part, part, cross_send.at[1], cross_recv.at[1], device(across))
    lax.fori_loop(x * 2, x * 2 + 2, heads, 0)
    ring_second(0, 1)

    def quad_part(who, y_at):
        return core_quad.at[
            pl.ds(pl.multiple_of(y_at * HEAD, HEAD), HEAD), pl.ds(pl.multiple_of(who * SEQ, SEQ), SEQ)
        ]

    def head_rows(ref, h):
        return ref.at[pl.ds(pl.multiple_of(h * HEAD, HEAD), HEAD)]

    def hand_out(k, ref, base, who):
        for yy in range(4):
            send(
                head_rows(ref, base + 2 * yy + 1 - c), quad_part(who, yy),
                quad_send.at[k, yy], quad_recv.at[k, yy], device(sibling),
            )
            quad_part(who, yy)[...] = head_rows(ref, base + 2 * yy + c)[...]

    hand_out(0, core_t, x * 8, member)
    arrived(across_t, cross_recv.at[0])
    hand_out(1, across_t, 0, member_across)

    def partial_at(shift, start, size):
        return partial.at[
            pl.ds(pl.multiple_of(lax.rem(y + shift + 4, 4) * BLOCK, BLOCK), BLOCK), pl.ds(start, size)
        ]

    def take_grad(j):
        arrived(grad_part(member_sibling, j), grad_recv.at[1, j])
        arrived(grad_part(member_corner, j), grad_recv.at[2, j])

    def partial_chunk(j):
        at = pl.ds(j * CHUNK, CHUNK)
        total = jnp.dot(core_quad[...], grad_quad[:, at], preferred_element_type=F32)
        partial[:, at] = (total * SCALE).astype(BF16)
        start, half = j * CHUNK, pl.ds(j * HALF, HALF)
        send(
            partial_at(2, start, HALF), relay_up.at[:, half],
            relay_send.at[0, j], relay_recv.at[0, j], device(up),
        )
        send(
            partial_at(2, start + HALF, HALF), relay_down.at[:, half],
            relay_send.at[1, j], relay_recv.at[1, j], device(down),
        )

    def relay_chunk(j):
        start, at, half = j * CHUNK, pl.ds(j * CHUNK, CHUNK), pl.ds(j * HALF, HALF)
        for shift, relay, k, place in ((1, relay_up, 0, start), (-1, relay_down, 1, start + HALF)):
            arrived(relay.at[:, half], relay_recv.at[k, j])
            spot = partial_at(shift, place, HALF)
            spot[...] = (spot[...].astype(F32) + relay[:, half].astype(F32)).astype(BF16)
        send(partial_at(1, start, CHUNK), sum_up.at[:, at], sum_send.at[0, j], sum_recv.at[0, j], device(up))
        send(partial_at(-1, start, CHUNK), sum_down.at[:, at], sum_send.at[1, j], sum_recv.at[1, j], device(down))

    power = jnp.full((1, 128), exponents[0, 0], jnp.int32).astype(F32)
    down_scale, up_scale = jnp.exp2(-power)[:, :1], jnp.exp2(power)[:, :1]

    def update_chunk(j):
        at = pl.ds(j * CHUNK, CHUNK)
        arrived(sum_up.at[:, at], sum_recv.at[0, j])
        arrived(sum_down.at[:, at], sum_recv.at[1, j])
        grad = partial_at(0, j * CHUNK, CHUNK)[...].astype(F32)
        grad = grad + sum_up[:, at].astype(F32) + sum_down[:, at].astype(F32)
        weight, base = weights[:, at], anchor[:, at]
        one = 0.9 * first[:, at] + 0.1 * grad
        two = 0.95 * second[:, at] + 0.05 * grad * grad
        updated = weight - 0.03 * (one / (jnp.sqrt(two) + 1e-08) + 0.1 * weight)
        encoded = jnp.clip((base - updated) * down_scale, -448.0, 448.0).astype(BF16)
        decoded[:, at] = (encoded.astype(F32) * up_scale).astype(BF16)
        if j % SENDS == SENDS - 1:
            group = j // SENDS
            span = pl.ds(group * SPAN, SPAN)
            for k, zz in enumerate(others):
                send(
                    decoded.at[pl.ds(pl.multiple_of(zz * SHARE, SHARE), SHARE), span], shares.at[z, :, span],
                    share_send.at[k, group], share_recv.at[z, group], replica_at(half, zz),
                )

    def share_rows(zz):
        return pl.ds(pl.multiple_of(zz * SHARE, SHARE), SHARE)

    def share_group(group):
        span = pl.ds(group * SPAN, SPAN)
        for zz in others:
            arrived(shares.at[zz, :, span], share_recv.at[zz, group])
        shares[z, :, span] = decoded[share_rows(z), span]
        total = shares[0, :, span].astype(F32)
        for zz in range(1, 4):
            total = total + shares[zz, :, span].astype(F32)
        halves[half, :, span] = total.astype(BF16)
        send(
            halves.at[half, :, span], halves.at[half, :, span],
            half_send.at[group], half_recv.at[group], replica_at(1 - half, z),
        )

    def outer_group(group):
        span = pl.ds(group * SPAN, SPAN)
        arrived(halves.at[1 - half, :, span], half_recv.at[group])
        total = halves[0, :, span].astype(F32) + halves[1, :, span].astype(F32)
        outer[share_rows(z), span] = (total * (1.0 / REPLICAS)).astype(BF16)
        part = outer.at[share_rows(z), span]
        for k, zz in enumerate(others):
            send(part, part, outer_send.at[k, group], outer_recv.at[z, group], replica_at(half, zz), late)

    def product_across():
        for h in range(8):
            across_n[:, h * HEAD : (h + 1) * HEAD] = (
                across_t[h * HEAD : (h + 1) * HEAD, :].astype(F32).T.astype(BF16)
            )

        def tile(n, carry):
            at = pl.multiple_of(n * CHUNK, CHUNK)
            total = jnp.dot(
                across_n[...],
                every_weight[pl.ds(pl.multiple_of(x * 1024, 1024), 1024), pl.ds(SIDE + at, CHUNK)],
                preferred_element_type=F32,
            )
            out_sent[:, pl.ds(at, CHUNK)] = (total * SCALE).astype(BF16)
            return carry

        lax.fori_loop(0, SIDE // CHUNK, tile, 0)

    def send_product(k):
        at = pl.ds(k * CHUNK, CHUNK)
        send(out_sent.at[:, at], out_across.at[:, at], out_send.at[k], out_recv.at[k], device(across), late)

    for j in range(EARLY):
        pass_grad(j)
    for n in range(6, 11):
        loads[n].wait()
    for yy in range(4):
        arrived(quad_part(member_sibling, yy), quad_recv.at[0, yy])
        arrived(quad_part(member_corner, yy), quad_recv.at[1, yy])

    for j in range(CHUNKS):
        take_grad(j)
        partial_chunk(j)
        if j >= 2:
            update_chunk(j - 2)
        if j >= 1:
            relay_chunk(j - 1)
        if EARLY <= j + 1 < CHUNKS:
            pass_grad(j + 1)
        if j == 2:
            share_near(0, 0)
            share_near(0, 1)
        if j == 3:
            share_far(0, 0)
            share_far(0, 1)
        if j == 4:
            for k in range(4):
                from_sibling(0, 1, k)
            product_across()
            send_product(0)
        if j >= 6:
            share_group(j - 6)
    relay_chunk(CHUNKS - 1)
    update_chunk(CHUNKS - 2)
    share_group(2)
    update_chunk(CHUNKS - 1)
    arrived(weight_side(across, 0), cross_recv.at[1])
    ring_first(1, 0, 0)
    ring_first(1, 0, 1)
    share_weight(1, 0, 0, across)
    share_group(3)
    for k in range(1, SIDE // CHUNK):
        send_product(k)
    for group in range(3):
        outer_group(group)

    def multiply(tiles, spots, size, begin, finish):
        def tile(n, carry):
            at = pl.ds(pl.multiple_of(n * CHUNK, CHUNK), CHUNK)
            total = None
            for spot in spots:
                term = jnp.dot(
                    core[:, pl.ds(spot, size)], every_weight[pl.ds(spot, size), at],
                    preferred_element_type=F32,
                )
                total = term if total is None else total + term
            if not begin:
                total = total + jnp.concatenate((first[:, at], second[:, at]), axis=0)
            if finish:
                partial[0:SEQ, at] = (total * SCALE).astype(BF16)
            else:
                first[:, at] = total[:BLOCK]
                second[:, at] = total[BLOCK:]
            return carry

        lax.fori_loop(tiles[0], tiles[1], tile, 0)

    def store_out(k):
        at = pl.ds(0, SIDE) if k == 0 else pl.ds(SIDE + (k - 1) * CHUNK, CHUNK)
        return pltpu.make_async_copy(partial.at[0:SEQ, at], layer_out_hbm.at[:, at], store_sem.at[2 + k])

    for k in range(4):
        from_sibling(0, 0, k)
    multiply((0, CHUNKS), [pl.multiple_of(x * 1024, 1024)], 1024, True, False)
    outer_group(3)
    ring_second(1, 0)
    for item in started:
        item.wait_send()

    def outer_step(zz):
        spot = share_rows(zz)
        delta = outer[spot, :].astype(F32)
        moved = 0.9 * momentum[spot, :] + delta
        momentum[spot, :] = moved
        anchor[spot, :] = anchor[spot, :] - 0.7 * (delta + 0.9 * moved)

    outer_step(z)
    for zz in others:
        for group in range(CHUNKS // SENDS):
            arrived(outer.at[share_rows(zz), pl.ds(group * SPAN, SPAN)], outer_recv.at[zz, group])
        outer_step(zz)
    stores = [
        pltpu.make_async_copy(anchor, new_anchor_hbm, store_sem.at[0]),
        pltpu.make_async_copy(momentum, new_momentum_hbm, store_sem.at[1]),
    ]
    for store in stores:
        store.start()

    share_near(1, 0)
    share_far(1, 0)
    for k in range(4):
        from_sibling(1, 0, k)
    multiply((0, CHUNKS // 2), [pl.multiple_of((1 - x) * 1024, 1024)], 1024, False, True)
    outs = [store_out(k) for k in range(5)]
    outs[0].start()
    for k in range(SIDE // CHUNK):
        part, at = pl.ds(k * CHUNK, CHUNK), pl.ds(SIDE + k * CHUNK, CHUNK)
        arrived(out_across.at[:, part], out_recv.at[k])
        for ref, spot in ((first, pl.ds(0, BLOCK)), (second, pl.ds(BLOCK, BLOCK))):
            partial[spot, at] = (ref[:, at] * SCALE + out_across[spot, part].astype(F32)).astype(BF16)
        outs[k + 1].start()
    for item in late:
        item.wait_send()
    for store in stores:
        store.wait()
    for out in outs:
        out.wait()


def on_device(
    queries, keys, values, log_decay, write_strength, out_grad, replica_weights,
    adam_first, adam_second, anchor, outer_momentum, exponents,
):
    dma = pltpu.SemaphoreType.DMA
    scratch = [
        pltpu.VMEM((SEQ, WIDTH), BF16),
        pltpu.VMEM((SEQ, WIDTH), BF16),
        pltpu.VMEM((SEQ, WIDTH), BF16),
        pltpu.VMEM((HEADS, SEQ), F32),
        pltpu.VMEM((HEADS, SEQ), F32),
        pltpu.VMEM((BLOCK, D), F32),
        pltpu.VMEM((BLOCK, D), F32),
        pltpu.VMEM((BLOCK, D), F32),
        pltpu.VMEM((BLOCK, D), F32),
        pltpu.VMEM((BLOCK, D), F32),
        pltpu.VMEM((GROUPS, 128, SEQ), F32),
        pltpu.VMEM((GROUPS, SEQ, 128), F32),
        pltpu.VMEM((SEQ, WIDTH), BF16),
        pltpu.VMEM((WIDTH, SEQ), BF16),
        pltpu.VMEM((WIDTH // 2, SEQ), BF16),
        pltpu.VMEM((SEQ, WIDTH // 2), BF16),
        pltpu.VMEM((SEQ, SIDE), BF16),
        pltpu.VMEM((SEQ, SIDE), BF16),
        pltpu.VMEM((4 * HEAD, 4 * SEQ), BF16),
        pltpu.VMEM((4 * SEQ, D), BF16),
        pltpu.VMEM((WIDTH, D), BF16),
        pltpu.VMEM((4 * BLOCK, D), BF16),
        pltpu.VMEM((BLOCK, SIDE), BF16),
        pltpu.VMEM((BLOCK, SIDE), BF16),
        pltpu.VMEM((BLOCK, D), BF16),
        pltpu.VMEM((BLOCK, D), BF16),
        pltpu.VMEM((BLOCK, D), BF16),
        pltpu.VMEM((4, SHARE, D), BF16),
        pltpu.VMEM((2, SHARE, D), BF16),
        pltpu.VMEM((BLOCK, D), BF16),
        dma((11,)), dma((7,)),
        dma((3, CHUNKS)), dma((3, CHUNKS)),
        dma((2, 4)), dma((2, 4)),
        dma((2, 2, 6)), dma((2, 2, 6)),
        dma((2, 2, 4)), dma((2, 2, 4)),
        dma((2,)), dma((2,)),
        dma((4,)), dma((4,)),
        dma((2, CHUNKS)), dma((2, CHUNKS)),
        dma((2, CHUNKS)), dma((2, CHUNKS)),
        dma((3, 4)), dma((4, 4)),
        dma((4,)), dma((4,)),
        dma((3, 4)), dma((4, 4)),
    ]
    anywhere = pl.BlockSpec(memory_space=pl.ANY)
    return pl.pallas_call(
        kernel,
        out_shape=(
            jax.ShapeDtypeStruct((SEQ, D), BF16),
            jax.ShapeDtypeStruct((BLOCK, D), F32),
            jax.ShapeDtypeStruct((BLOCK, D), F32),
        ),
        in_specs=[anywhere] * 11 + [pl.BlockSpec(memory_space=pltpu.SMEM)],
        out_specs=(anywhere,) * 3,
        scratch_shapes=scratch,
        compiler_params=pltpu.CompilerParams(
            collective_id=0, has_side_effects=True, vmem_limit_bytes=60 * 1024 * 1024
        ),
        name="diloco_step",
    )(
        queries, keys, values, log_decay, write_strength, out_grad, replica_weights,
        adam_first, adam_second, anchor, outer_momentum, exponents,
    )


def solution(mesh):
    return jax.shard_map(
        on_device,
        mesh=mesh,
        in_specs=(
            P(("replica", "fsdp"), None),
            P(("replica", "fsdp"), None),
            P(("replica", "fsdp"), None),
            P(None, ("replica", "fsdp")),
            P(None, ("replica", "fsdp")),
            P(("replica", "fsdp"), None),
            P("replica", "fsdp", None),
            P("replica", "fsdp", None),
            P("replica", "fsdp", None),
            P("fsdp", None),
            P("fsdp", None),
            P("replica", "fsdp"),
        ),
        out_specs=(P(("replica", "fsdp"), None), P("fsdp", None), P("fsdp", None)),
        check_vma=False,
    )
```

```python
import jax
import jax.numpy as jnp
from jax import lax
from jax.experimental import pallas as pl
from jax.experimental.pallas import tpu as pltpu
from jax.sharding import PartitionSpec as P

HEAD = 128
HEADS = 16
SEQ = 256
WIDTH = HEADS * HEAD
D = 4096
BLOCK = 128
REPLICAS = 8
SHARE = BLOCK // 4
GROUP = 4
GROUPS = HEADS // GROUP
CHUNK = 512
CHUNKS = D // CHUNK
HALF = CHUNK // 2
SIDE = D // 2
PIECES = (((0, 2048), (2048, 2048)), ((0, 2048),))
WHOLE = 2048
SHARED = D - WHOLE
TILE = 512
OUTS = ((0, 2048), (2048, 512), (2560, 512), (3072, 512), (3584, 512))
SCALE = WIDTH ** (-0.5)
EARLY = 2
SENDS = 2
SPAN = SENDS * CHUNK
F32 = jnp.float32
BF16 = jnp.bfloat16
NT = (((1,), (1,)), ((), ()))
MESH = pl.DeviceIdType.MESH


def split(item):
    high = item.astype(BF16)
    return high, (item - high.astype(F32)).astype(BF16)


def as_left(item):
    return jnp.concatenate(split(item), axis=1)


def as_right(item):
    row = jnp.concatenate(split(item), axis=1)
    return jnp.concatenate((row, row), axis=0)


def product(left, right):
    both = jnp.dot(left, right, preferred_element_type=F32)
    return both[:, :HEAD] + both[:, HEAD:]


def fill_tables(keys, log_decay, strength, rows, cols):
    i = lax.broadcasted_iota(jnp.int32, (SEQ, SEQ), 0)
    j = lax.broadcasted_iota(jnp.int32, (SEQ, SEQ), 1)
    upto = jnp.where(i <= j, 1.0, 0.0).astype(F32)
    sums = jnp.dot(
        log_decay[...], upto, preferred_element_type=F32, precision=lax.Precision.HIGHEST
    )
    ones = jnp.ones((8, HEAD), BF16)
    rows[...] = jnp.zeros_like(rows)
    for g in range(GROUPS):
        rows[g, 0:GROUP, :] = sums[g * GROUP : (g + 1) * GROUP]
        rows[g, GROUP : 2 * GROUP, :] = strength[g * GROUP : (g + 1) * GROUP, :]
        for n in range(GROUP):
            h = g * GROUP + n
            key = keys[:, h * HEAD : (h + 1) * HEAD].astype(F32)
            high, low = split(key * key)
            total = lax.dot_general(ones, high, NT, preferred_element_type=F32)
            total = total + lax.dot_general(ones, low, NT, preferred_element_type=F32)
            rows[g, 2 * GROUP + n : 2 * GROUP + n + 1, :] = lax.rsqrt(total[0:1] + 1e-6)
        cols[g] = rows[g].T


def delta_group(g, queries, keys, values, rows, cols):
    i = lax.broadcasted_iota(jnp.int32, (HEAD, HEAD), 0)
    j = lax.broadcasted_iota(jnp.int32, (HEAD, HEAD), 1)
    col = cols[g]
    low, strict = i >= j, i > j
    couple_1, couple_2, cross, mix_1, mix_2, mix_cross, sides = [], [], [], [], [], [], []
    for n in range(GROUP):
        at = pl.ds(pl.multiple_of((g * GROUP + n) * HEAD, HEAD), HEAD)
        query, key = queries[:, at], keys[:, at]
        decay_row = rows[g, n : n + 1, :]
        norm_row = rows[g, 2 * GROUP + n : 2 * GROUP + n + 1, :]
        decay_col = col[:, n : n + 1]
        strength = col[:, GROUP + n : GROUP + n + 1]
        scaled = strength * col[:, 2 * GROUP + n : 2 * GROUP + n + 1]
        dots = lax.dot_general(
            jnp.concatenate((key, query), axis=0), key, NT, preferred_element_type=F32
        )
        left_norm, right_norm = norm_row[:, :HEAD], norm_row[:, HEAD:]
        gap_1 = decay_col[:HEAD] - decay_row[:, :HEAD]
        gap_2 = decay_col[HEAD:] - decay_row[:, HEAD:]
        gap_cross = decay_col[HEAD:] - decay_row[:, :HEAD]
        fade_1 = jnp.exp(jnp.where(low, gap_1, -1e30)) * left_norm
        fade_2 = jnp.exp(jnp.where(low, gap_2, -1e30)) * right_norm
        fade_cross = jnp.exp(jnp.minimum(gap_cross, 0.0)) * left_norm
        couple_1.append(jnp.where(strict, dots[:HEAD, :HEAD] * fade_1 * scaled[:HEAD], 0.0))
        couple_2.append(jnp.where(strict, dots[HEAD:SEQ, HEAD:] * fade_2 * scaled[HEAD:], 0.0))
        cross.append(dots[HEAD:SEQ, :HEAD] * fade_cross * scaled[HEAD:])
        size = HEAD ** (-0.5)
        mix_1.append(dots[SEQ : SEQ + HEAD, :HEAD] * fade_1 * size)
        mix_2.append(dots[SEQ + HEAD :, HEAD:] * fade_2 * size)
        mix_cross.append(dots[SEQ + HEAD :, :HEAD] * fade_cross * size)
        sides.append(strength * values[:, at].astype(F32))
    couples = couple_1 + couple_2
    eye = jnp.where(i == j, 1.0, 0.0).astype(F32)
    inverse = [eye - jnp.where(i // 2 == j // 2, couple, 0.0) for couple in couples]
    size = 2
    while size < HEAD:
        below = (i // (2 * size) == j // (2 * size)) & (i % (2 * size) >= size) & (j % (2 * size) < size)
        lefts = [as_left(jnp.where(below, couple, 0.0)) for couple in couples]
        steps = [product(left, as_right(item)) for left, item in zip(lefts, inverse)]
        inverse = [item - product(as_left(item), as_right(step)) for item, step in zip(inverse, steps)]
        size *= 2
    results = []
    fresh_1 = [product(as_left(inverse[n]), as_right(sides[n][:HEAD])) for n in range(GROUP)]
    uses = [
        product(
            as_left(jnp.concatenate((cross[n], mix_1[n], mix_cross[n]), axis=0)), as_right(fresh_1[n])
        )
        for n in range(GROUP)
    ]
    fresh_2 = [
        product(as_left(inverse[GROUP + n]), as_right(sides[n][HEAD:] - uses[n][:HEAD]))
        for n in range(GROUP)
    ]
    for n in range(GROUP):
        second = uses[n][2 * HEAD :] + product(as_left(mix_2[n]), as_right(fresh_2[n]))
        results.append(jnp.concatenate((uses[n][HEAD : 2 * HEAD], second), axis=0))
    return results


def kernel(
    queries_hbm, keys_hbm, values_hbm, decay_hbm, strength_hbm, out_grad_hbm, weights_hbm,
    first_hbm, second_hbm, anchor_hbm, momentum_hbm, exponents,
    layer_out_hbm, state_hbm,
    queries, keys, values, decay, strength, weights, first, second, anchor, momentum,
    rows, cols, core, core_t, across_t, across_n, out_sent, out_across, core_quad, grad_quad, every_weight, partial,
    relay_up, relay_down, sum_up, sum_down, decoded, shares, halves, outer,
    load_sem, store_sem, grad_send, grad_recv, quad_send, quad_recv, row_send, row_recv,
    pair_send, pair_recv, cross_send, cross_recv, out_send, out_recv, relay_send, relay_recv, sum_send, sum_recv,
    share_send, share_recv, half_send, half_recv, outer_send, outer_recv,
):
    replica, me = lax.axis_index("replica"), lax.axis_index("fsdp")
    x, y, c = me // 8, (me // 2) % 4, me % 2

    def index(x_at, y_at, c_at):
        return x_at * 8 + lax.rem(y_at + 4, 4) * 2 + c_at

    def device(f):
        return {"replica": replica, "fsdp": f}

    sibling, across, corner = index(x, y, 1 - c), index(1 - x, y, c), index(1 - x, y, 1 - c)
    up, down = index(x, y + 1, c), index(x, y - 1, c)
    z = lax.rem(replica, 4)
    half = replica // 4
    others = [lax.rem(z + k, 4) for k in range(1, 4)]

    def replica_at(half_at, z_at):
        return {"replica": half_at * 4 + z_at, "fsdp": me}

    member = x * 2 + c
    member_sibling, member_across, member_corner = x * 2 + 1 - c, (1 - x) * 2 + c, (1 - x) * 2 + 1 - c

    started, late = [], []

    def copy(src, dst, send_sem, recv_sem, to):
        return pltpu.make_async_remote_copy(
            src_ref=src, dst_ref=dst, send_sem=send_sem, recv_sem=recv_sem,
            device_id=to, device_id_type=MESH,
        )

    def send(src, dst, send_sem, recv_sem, to, kept=started):
        item = copy(src, dst, send_sem, recv_sem, to)
        item.start()
        kept.append(item)

    def arrived(region, recv_sem):
        copy(region, region, recv_sem, recv_sem, device(sibling)).wait_recv()

    grad_own = grad_quad.at[pl.ds(pl.multiple_of(member * SEQ, SEQ), SEQ)]
    loads = [
        (weights_hbm.at[0], weights), (keys_hbm, keys), (decay_hbm, decay), (strength_hbm, strength),
        (queries_hbm, queries), (values_hbm, values), (out_grad_hbm, grad_own), (first_hbm.at[0], first),
        (second_hbm.at[0], second), (anchor_hbm, anchor), (momentum_hbm, momentum),
    ]
    loads = [pltpu.make_async_copy(src, dst, load_sem.at[n]) for n, (src, dst) in enumerate(loads)]
    barrier = pltpu.get_barrier_semaphore()
    peers = [device(f) for f in (sibling, across, corner, up, down)]
    peers += [replica_at(half, zz) for zz in others] + [replica_at(1 - half, z)]
    for peer in peers:
        pl.semaphore_signal(barrier, inc=1, device_id=peer, device_id_type=MESH)
    for load in loads[:6]:
        load.start()
    pl.semaphore_wait(barrier, len(peers))

    def weight_rows(f):
        return every_weight.at[pl.ds(pl.multiple_of(f * BLOCK, BLOCK), BLOCK)]

    def grad_part(who, j):
        return grad_quad.at[
            pl.ds(pl.multiple_of(who * SEQ, SEQ), SEQ), pl.ds(j * CHUNK, CHUNK)
        ]

    def send_grad(j):
        src = out_grad_hbm.at[:, pl.ds(j * CHUNK, CHUNK)]
        send(src, grad_part(member, j), grad_send.at[0, j], grad_recv.at[0, j], device(across))
        send(src, grad_part(member, j), grad_send.at[1, j], grad_recv.at[1, j], device(sibling))

    def pass_grad(j):
        arrived(grad_part(member_across, j), grad_recv.at[0, j])
        send(
            grad_part(member_across, j), grad_part(member_across, j),
            grad_send.at[2, j], grad_recv.at[2, j], device(sibling),
        )

    def weight_part(f, start, size):
        return every_weight.at[
            pl.ds(pl.multiple_of(f * BLOCK, BLOCK), BLOCK), pl.ds(start, size)
        ]

    def weight_piece(u, p, f):
        return weight_part(f, *PIECES[u][p])

    def weight_half(u, p, f, side):
        start, size = PIECES[u][p]
        return weight_part(f, start + side * size // 2, size // 2)

    def ring(u, p, k, f, side, to):
        part = weight_half(u, p, f, side)
        send(part, part, row_send.at[u, p, k], row_recv.at[u, p, k], device(to), (started, late)[u])

    def ring_arrived(u, p, k, f, side):
        arrived(weight_half(u, p, f, side), row_recv.at[u, p, k])

    def share_weight(u, p, k, f):
        part = weight_piece(u, p, f)
        send(part, part, pair_send.at[u, p, k], pair_recv.at[u, p, k], device(sibling), (started, late)[u])

    def cross_weight(p):
        part = weight_piece(1, p, me)
        send(part, part, cross_send.at[1 + p], cross_recv.at[1 + p], device(across))

    def take_weight(p):
        arrived(weight_piece(1, p, across), cross_recv.at[1 + p])
        ring_first(1, p, 0)
        ring_first(1, p, 1)
        share_weight(1, p, 0, across)

    column = (x, 1 - x)

    def ring_first(u, p, step):
        block = index(column[u], y, c)
        ring(u, p, 2 * step, block, step, up)
        ring(u, p, 2 * step + 1, block, 1 - step, down)

    def ring_second(u, p):
        below, above = index(column[u], y - 1, c), index(column[u], y + 1, c)
        ring_arrived(u, p, 0, below, 0)
        ring(u, p, 4, below, 0, up)
        ring_arrived(u, p, 1, above, 1)
        ring(u, p, 5, above, 1, down)

    def share_near(u, p):
        below, above = index(column[u], y - 1, c), index(column[u], y + 1, c)
        ring_arrived(u, p, 2, below, 1)
        share_weight(u, p, 1, below)
        ring_arrived(u, p, 3, above, 0)
        share_weight(u, p, 2, above)

    def share_far(u, p):
        far = index(column[u], y + 2, c)
        ring_arrived(u, p, 4, far, 0)
        ring_arrived(u, p, 5, far, 1)
        share_weight(u, p, 3, far)

    def from_sibling(u, p, k):
        shift = (0, -1, 1, 2)[k]
        arrived(weight_piece(u, p, index(column[u], y + shift, 1 - c)), pair_recv.at[u, p, k])

    for j in range(EARLY):
        send_grad(j)
    loads[0].wait()
    for p in range(2):
        start, size = PIECES[0][p]
        weight_piece(0, p, me)[...] = weights[:, start : start + size].astype(BF16)
        ring_first(0, p, 0)
        ring_first(0, p, 1)
    for p in range(2):
        share_weight(0, p, 0, me)
    for load in loads[6:]:
        load.start()

    for n in range(1, 6):
        loads[n].wait()
    fill_tables(keys, decay, strength, rows, cols)

    def heads(g, carry):
        results = delta_group(g, queries, keys, values, rows, cols)
        for n, result in enumerate(results):
            at = pl.ds(pl.multiple_of((g * GROUP + n) * HEAD, HEAD), HEAD)
            core[:, at] = result.astype(BF16)
            core_t[at, :] = result.T.astype(BF16)
        return carry

    lax.fori_loop((1 - x) * 2, (1 - x) * 2 + 2, heads, 0)
    ring_second(0, 0)
    other_rows = core_t.at[pl.ds(pl.multiple_of((1 - x) * 1024, 1024), 1024)]
    send(other_rows, across_t, cross_send.at[0], cross_recv.at[0], device(across))
    for j in range(EARLY, CHUNKS):
        send_grad(j)
    cross_weight(0)
    lax.fori_loop(x * 2, x * 2 + 2, heads, 0)
    ring_second(0, 1)

    def quad_part(who, y_at):
        return core_quad.at[
            pl.ds(pl.multiple_of(y_at * HEAD, HEAD), HEAD), pl.ds(pl.multiple_of(who * SEQ, SEQ), SEQ)
        ]

    def head_rows(ref, h):
        return ref.at[pl.ds(pl.multiple_of(h * HEAD, HEAD), HEAD)]

    def hand_out(k, ref, base, who):
        for yy in range(4):
            send(
                head_rows(ref, base + 2 * yy + 1 - c), quad_part(who, yy),
                quad_send.at[k, yy], quad_recv.at[k, yy], device(sibling),
            )
            quad_part(who, yy)[...] = head_rows(ref, base + 2 * yy + c)[...]

    hand_out(0, core_t, x * 8, member)
    arrived(across_t, cross_recv.at[0])
    hand_out(1, across_t, 0, member_across)

    def partial_at(shift, start, size):
        return partial.at[
            pl.ds(pl.multiple_of(lax.rem(y + shift + 4, 4) * BLOCK, BLOCK), BLOCK), pl.ds(start, size)
        ]

    def take_grad(j):
        arrived(grad_part(member_sibling, j), grad_recv.at[1, j])
        arrived(grad_part(member_corner, j), grad_recv.at[2, j])

    def partial_chunk(j):
        at = pl.ds(j * CHUNK, CHUNK)
        total = jnp.dot(core_quad[...], grad_quad[:, at], preferred_element_type=F32)
        partial[:, at] = (total * SCALE).astype(BF16)
        start, half = j * CHUNK, pl.ds(j * HALF, HALF)
        send(
            partial_at(2, start, HALF), relay_up.at[:, half],
            relay_send.at[0, j], relay_recv.at[0, j], device(up),
        )
        send(
            partial_at(2, start + HALF, HALF), relay_down.at[:, half],
            relay_send.at[1, j], relay_recv.at[1, j], device(down),
        )

    def relay_chunk(j):
        start, at, half = j * CHUNK, pl.ds(j * CHUNK, CHUNK), pl.ds(j * HALF, HALF)
        for shift, relay, k, place in ((1, relay_up, 0, start), (-1, relay_down, 1, start + HALF)):
            arrived(relay.at[:, half], relay_recv.at[k, j])
            spot = partial_at(shift, place, HALF)
            spot[...] = (spot[...].astype(F32) + relay[:, half].astype(F32)).astype(BF16)
        send(partial_at(1, start, CHUNK), sum_up.at[:, at], sum_send.at[0, j], sum_recv.at[0, j], device(up))
        send(partial_at(-1, start, CHUNK), sum_down.at[:, at], sum_send.at[1, j], sum_recv.at[1, j], device(down))

    power = jnp.full((1, 128), exponents[0, 0], jnp.int32).astype(F32)
    down_scale, up_scale = jnp.exp2(-power)[:, :1], jnp.exp2(power)[:, :1]

    def update_chunk(j):
        at = pl.ds(j * CHUNK, CHUNK)
        arrived(sum_up.at[:, at], sum_recv.at[0, j])
        arrived(sum_down.at[:, at], sum_recv.at[1, j])
        grad = partial_at(0, j * CHUNK, CHUNK)[...].astype(F32)
        grad = grad + sum_up[:, at].astype(F32) + sum_down[:, at].astype(F32)
        weight, base = weights[:, at], anchor[:, at]
        one = 0.9 * first[:, at] + 0.1 * grad
        two = 0.95 * second[:, at] + 0.05 * grad * grad
        updated = weight - 0.03 * (one / (jnp.sqrt(two) + 1e-08) + 0.1 * weight)
        encoded = jnp.clip((base - updated) * down_scale, -448.0, 448.0).astype(BF16)
        decoded[:, at] = (encoded.astype(F32) * up_scale).astype(BF16)
        if j % SENDS == SENDS - 1:
            group = j // SENDS
            span = pl.ds(group * SPAN, SPAN)
            for k, zz in enumerate(others):
                send(
                    decoded.at[pl.ds(pl.multiple_of(zz * SHARE, SHARE), SHARE), span], shares.at[z, :, span],
                    share_send.at[k, group], share_recv.at[z, group], replica_at(half, zz),
                )

    def share_rows(zz):
        return pl.ds(pl.multiple_of(zz * SHARE, SHARE), SHARE)

    def share_group(group):
        span = pl.ds(group * SPAN, SPAN)
        for zz in others:
            arrived(shares.at[zz, :, span], share_recv.at[zz, group])
        shares[z, :, span] = decoded[share_rows(z), span]
        total = shares[0, :, span].astype(F32)
        for zz in range(1, 4):
            total = total + shares[zz, :, span].astype(F32)
        halves[half, :, span] = total.astype(BF16)
        send(
            halves.at[half, :, span], halves.at[half, :, span],
            half_send.at[group], half_recv.at[group], replica_at(1 - half, z),
        )

    def outer_group(group):
        span = pl.ds(group * SPAN, SPAN)
        arrived(halves.at[1 - half, :, span], half_recv.at[group])
        total = halves[0, :, span].astype(F32) + halves[1, :, span].astype(F32)
        outer[share_rows(z), span] = (total * (1.0 / REPLICAS)).astype(BF16)
        part = outer.at[share_rows(z), span]
        for k, zz in enumerate(others):
            send(part, part, outer_send.at[k, group], outer_recv.at[z, group], replica_at(half, zz), late)

    def product_across():
        for h in range(8):
            across_n[:, h * HEAD : (h + 1) * HEAD] = (
                across_t[h * HEAD : (h + 1) * HEAD, :].astype(F32).T.astype(BF16)
            )

        def tile(n, carry):
            at = pl.multiple_of(n * TILE, TILE)
            total = jnp.dot(
                across_n[...],
                every_weight[pl.ds(pl.multiple_of(x * 1024, 1024), 1024), pl.ds(WHOLE + at, TILE)],
                preferred_element_type=F32,
            )
            out_sent[:, pl.ds(at, TILE)] = (total * SCALE).astype(BF16)
            return carry

        lax.fori_loop(0, SHARED // TILE, tile, 0)

    def send_product(k):
        start, size = OUTS[1 + k]
        at = pl.ds(start - WHOLE, size)
        send(out_sent.at[:, at], out_across.at[:, at], out_send.at[k], out_recv.at[k], device(across), late)

    for j in range(EARLY):
        pass_grad(j)
    for n in range(6, 11):
        loads[n].wait()
    for yy in range(4):
        arrived(quad_part(member_sibling, yy), quad_recv.at[0, yy])
        arrived(quad_part(member_corner, yy), quad_recv.at[1, yy])

    for j in range(CHUNKS):
        take_grad(j)
        partial_chunk(j)
        if j >= 2:
            update_chunk(j - 2)
        if j >= 1:
            relay_chunk(j - 1)
        if EARLY <= j + 1 < CHUNKS:
            pass_grad(j + 1)
        if j == 2:
            share_near(0, 0)
            share_near(0, 1)
        if j == 3:
            share_far(0, 0)
            share_far(0, 1)
        if j == 4:
            for k in range(4):
                from_sibling(0, 1, k)
            product_across()
            send_product(0)
        if j >= 6:
            share_group(j - 6)
    relay_chunk(CHUNKS - 1)
    update_chunk(CHUNKS - 2)
    share_group(2)
    update_chunk(CHUNKS - 1)
    take_weight(0)
    share_group(3)
    for k in range(1, 4):
        send_product(k)
    for group in range(3):
        outer_group(group)

    def multiply(tiles, spots, size, begin, finish):
        def tile(n, carry):
            at = pl.ds(pl.multiple_of(n * TILE, TILE), TILE)
            total = None
            for spot in spots:
                term = jnp.dot(
                    core[:, pl.ds(spot, size)], every_weight[pl.ds(spot, size), at],
                    preferred_element_type=F32,
                )
                total = term if total is None else total + term
            if not begin:
                total = total + jnp.concatenate((first[:, at], second[:, at]), axis=0)
            if finish:
                partial[0:SEQ, at] = (total * SCALE).astype(BF16)
            else:
                first[:, at] = total[:BLOCK]
                second[:, at] = total[BLOCK:]
            return carry

        lax.fori_loop(tiles[0], tiles[1], tile, 0)

    def store_out(k):
        start, size = OUTS[k]
        at = pl.ds(start, size)
        store = pltpu.make_async_copy(partial.at[0:SEQ, at], layer_out_hbm.at[:, at], store_sem.at[k])
        store.start()
        stores.append(store)

    def add_across(k):
        start, size = OUTS[1 + k]
        part, at = pl.ds(start - WHOLE, size), pl.ds(start, size)
        arrived(out_across.at[:, part], out_recv.at[k])
        for ref, spot in ((first, pl.ds(0, BLOCK)), (second, pl.ds(BLOCK, BLOCK))):
            partial[spot, at] = (ref[:, at] * SCALE + out_across[spot, part].astype(F32)).astype(BF16)
        store_out(1 + k)

    def outer_step(zz):
        spot = share_rows(zz)
        delta = outer[spot, :].astype(F32)
        moved = 0.9 * momentum[spot, :] + delta
        momentum[spot, :] = moved
        anchor[spot, :] = anchor[spot, :] - 0.7 * (delta + 0.9 * moved)

    stores = []
    for k in range(4):
        from_sibling(0, 0, k)
    multiply((0, D // TILE), [pl.multiple_of(x * 1024, 1024)], 1024, True, False)
    outer_group(3)
    ring_second(1, 0)
    for item in started:
        item.wait_send()
    outer_step(z)
    for zz in others:
        for group in range(CHUNKS // SENDS):
            arrived(outer.at[share_rows(zz), pl.ds(group * SPAN, SPAN)], outer_recv.at[zz, group])
        outer_step(zz)
    for n, ref in enumerate((anchor, momentum)):
        store = pltpu.make_async_copy(ref, state_hbm.at[n * BLOCK : (n + 1) * BLOCK], store_sem.at[6 + n])
        store.start()
        stores.append(store)
    share_near(1, 0)
    share_far(1, 0)
    for k in range(4):
        from_sibling(1, 0, k)
    multiply((0, WHOLE // TILE), [pl.multiple_of((1 - x) * 1024, 1024)], 1024, False, True)
    store_out(0)
    for k in range(4):
        add_across(k)
    for item in late:
        item.wait_send()
    for store in stores:
        store.wait()


def on_device(
    queries, keys, values, log_decay, write_strength, out_grad, replica_weights,
    adam_first, adam_second, anchor, outer_momentum, exponents,
):
    dma = pltpu.SemaphoreType.DMA
    scratch = [
        pltpu.VMEM((SEQ, WIDTH), BF16),
        pltpu.VMEM((SEQ, WIDTH), BF16),
        pltpu.VMEM((SEQ, WIDTH), BF16),
        pltpu.VMEM((HEADS, SEQ), F32),
        pltpu.VMEM((HEADS, SEQ), F32),
        pltpu.VMEM((BLOCK, D), F32),
        pltpu.VMEM((BLOCK, D), F32),
        pltpu.VMEM((BLOCK, D), F32),
        pltpu.VMEM((BLOCK, D), F32),
        pltpu.VMEM((BLOCK, D), F32),
        pltpu.VMEM((GROUPS, 128, SEQ), F32),
        pltpu.VMEM((GROUPS, SEQ, 128), F32),
        pltpu.VMEM((SEQ, WIDTH), BF16),
        pltpu.VMEM((WIDTH, SEQ), BF16),
        pltpu.VMEM((WIDTH // 2, SEQ), BF16),
        pltpu.VMEM((SEQ, WIDTH // 2), BF16),
        pltpu.VMEM((SEQ, SHARED), BF16),
        pltpu.VMEM((SEQ, SHARED), BF16),
        pltpu.VMEM((4 * HEAD, 4 * SEQ), BF16),
        pltpu.VMEM((4 * SEQ, D), BF16),
        pltpu.VMEM((WIDTH, D), BF16),
        pltpu.VMEM((4 * BLOCK, D), BF16),
        pltpu.VMEM((BLOCK, SIDE), BF16),
        pltpu.VMEM((BLOCK, SIDE), BF16),
        pltpu.VMEM((BLOCK, D), BF16),
        pltpu.VMEM((BLOCK, D), BF16),
        pltpu.VMEM((BLOCK, D), BF16),
        pltpu.VMEM((4, SHARE, D), BF16),
        pltpu.VMEM((2, SHARE, D), BF16),
        pltpu.VMEM((BLOCK, D), BF16),
        dma((11,)), dma((8,)),
        dma((3, CHUNKS)), dma((3, CHUNKS)),
        dma((2, 4)), dma((2, 4)),
        dma((2, 2, 6)), dma((2, 2, 6)),
        dma((2, 2, 4)), dma((2, 2, 4)),
        dma((3,)), dma((3,)),
        dma((4,)), dma((4,)),
        dma((2, CHUNKS)), dma((2, CHUNKS)),
        dma((2, CHUNKS)), dma((2, CHUNKS)),
        dma((3, 4)), dma((4, 4)),
        dma((4,)), dma((4,)),
        dma((3, 4)), dma((4, 4)),
    ]
    anywhere = pl.BlockSpec(memory_space=pl.ANY)
    layer_out, state = pl.pallas_call(
        kernel,
        out_shape=(
            jax.ShapeDtypeStruct((SEQ, D), BF16),
            jax.ShapeDtypeStruct((2 * BLOCK, D), F32),
        ),
        in_specs=[anywhere] * 11 + [pl.BlockSpec(memory_space=pltpu.SMEM)],
        out_specs=(anywhere,) * 2,
        scratch_shapes=scratch,
        compiler_params=pltpu.CompilerParams(
            collective_id=0, has_side_effects=True, vmem_limit_bytes=60 * 1024 * 1024
        ),
        name="diloco_step",
    )(
        queries, keys, values, log_decay, write_strength, out_grad, replica_weights,
        adam_first, adam_second, anchor, outer_momentum, exponents,
    )
    return layer_out, state[:BLOCK], state[BLOCK:]


def solution(mesh):
    return jax.shard_map(
        on_device,
        mesh=mesh,
        in_specs=(
            P(("replica", "fsdp"), None),
            P(("replica", "fsdp"), None),
            P(("replica", "fsdp"), None),
            P(None, ("replica", "fsdp")),
            P(None, ("replica", "fsdp")),
            P(("replica", "fsdp"), None),
            P("replica", "fsdp", None),
            P("replica", "fsdp", None),
            P("replica", "fsdp", None),
            P("fsdp", None),
            P("fsdp", None),
            P("replica", "fsdp"),
        ),
        out_specs=(P(("replica", "fsdp"), None), P("fsdp", None), P("fsdp", None)),
        check_vma=False,
    )
```

```python
import jax
import jax.numpy as jnp
from jax import lax
from jax.experimental import pallas as pl
from jax.experimental.pallas import tpu as pltpu
from jax.sharding import PartitionSpec as P

HEAD = 128
HEADS = 16
SEQ = 256
WIDTH = HEADS * HEAD
D = 4096
BLOCK = 128
REPLICAS = 8
SHARE = BLOCK // 4
GROUP = 4
GROUPS = HEADS // GROUP
CHUNK = 512
CHUNKS = D // CHUNK
HALF = CHUNK // 2
SIDE = D // 2
PIECES = (((0, 2048), (2048, 2048)), ((0, 2048),))
WHOLE = 2048
SHARED = D - WHOLE
TILE = 512
OUTS = ((0, 2048), (2048, 512), (2560, 512), (3072, 512), (3584, 512))
SCALE = WIDTH ** (-0.5)
EARLY = 2
SENDS = 2
SPAN = SENDS * CHUNK
F32 = jnp.float32
BF16 = jnp.bfloat16
NT = (((1,), (1,)), ((), ()))
MESH = pl.DeviceIdType.MESH


def split(item):
    high = item.astype(BF16)
    return high, (item - high.astype(F32)).astype(BF16)


def as_left(item):
    return jnp.concatenate(split(item), axis=1)


def as_right(item):
    row = jnp.concatenate(split(item), axis=1)
    return jnp.concatenate((row, row), axis=0)


def product(left, right):
    both = jnp.dot(left, right, preferred_element_type=F32)
    return both[:, :HEAD] + both[:, HEAD:]


def fill_tables(keys, log_decay, strength, rows, cols):
    i = lax.broadcasted_iota(jnp.int32, (SEQ, SEQ), 0)
    j = lax.broadcasted_iota(jnp.int32, (SEQ, SEQ), 1)
    upto = jnp.where(i <= j, 1.0, 0.0).astype(F32)
    sums = jnp.dot(
        log_decay[...], upto, preferred_element_type=F32, precision=lax.Precision.HIGHEST
    )
    ones = jnp.ones((8, HEAD), BF16)
    rows[...] = jnp.zeros_like(rows)
    for g in range(GROUPS):
        rows[g, 0:GROUP, :] = sums[g * GROUP : (g + 1) * GROUP]
        rows[g, GROUP : 2 * GROUP, :] = strength[g * GROUP : (g + 1) * GROUP, :]
        for n in range(GROUP):
            h = g * GROUP + n
            key = keys[:, h * HEAD : (h + 1) * HEAD].astype(F32)
            high, low = split(key * key)
            total = lax.dot_general(ones, high, NT, preferred_element_type=F32)
            total = total + lax.dot_general(ones, low, NT, preferred_element_type=F32)
            rows[g, 2 * GROUP + n : 2 * GROUP + n + 1, :] = lax.rsqrt(total[0:1] + 1e-6)
        cols[g] = rows[g].T


def delta_group(g, queries, keys, values, rows, cols):
    i = lax.broadcasted_iota(jnp.int32, (HEAD, HEAD), 0)
    j = lax.broadcasted_iota(jnp.int32, (HEAD, HEAD), 1)
    col = cols[g]
    low, strict = i >= j, i > j
    couple_1, couple_2, cross, mix_1, mix_2, mix_cross, sides = [], [], [], [], [], [], []
    for n in range(GROUP):
        at = pl.ds(pl.multiple_of((g * GROUP + n) * HEAD, HEAD), HEAD)
        query, key = queries[:, at], keys[:, at]
        decay_row = rows[g, n : n + 1, :]
        norm_row = rows[g, 2 * GROUP + n : 2 * GROUP + n + 1, :]
        decay_col = col[:, n : n + 1]
        strength = col[:, GROUP + n : GROUP + n + 1]
        scaled = strength * col[:, 2 * GROUP + n : 2 * GROUP + n + 1]
        dots = lax.dot_general(
            jnp.concatenate((key, query), axis=0), key, NT, preferred_element_type=F32
        )
        left_norm, right_norm = norm_row[:, :HEAD], norm_row[:, HEAD:]
        gap_1 = decay_col[:HEAD] - decay_row[:, :HEAD]
        gap_2 = decay_col[HEAD:] - decay_row[:, HEAD:]
        gap_cross = decay_col[HEAD:] - decay_row[:, :HEAD]
        fade_1 = jnp.exp(jnp.where(low, gap_1, -1e30)) * left_norm
        fade_2 = jnp.exp(jnp.where(low, gap_2, -1e30)) * right_norm
        fade_cross = jnp.exp(jnp.minimum(gap_cross, 0.0)) * left_norm
        couple_1.append(jnp.where(strict, dots[:HEAD, :HEAD] * fade_1 * scaled[:HEAD], 0.0))
        couple_2.append(jnp.where(strict, dots[HEAD:SEQ, HEAD:] * fade_2 * scaled[HEAD:], 0.0))
        cross.append(dots[HEAD:SEQ, :HEAD] * fade_cross * scaled[HEAD:])
        size = HEAD ** (-0.5)
        mix_1.append(dots[SEQ : SEQ + HEAD, :HEAD] * fade_1 * size)
        mix_2.append(dots[SEQ + HEAD :, HEAD:] * fade_2 * size)
        mix_cross.append(dots[SEQ + HEAD :, :HEAD] * fade_cross * size)
        sides.append(strength * values[:, at].astype(F32))
    couples = couple_1 + couple_2
    eye = jnp.where(i == j, 1.0, 0.0).astype(F32)
    inverse = [eye - jnp.where(i // 2 == j // 2, couple, 0.0) for couple in couples]
    size = 2
    while size < HEAD:
        below = (i // (2 * size) == j // (2 * size)) & (i % (2 * size) >= size) & (j % (2 * size) < size)
        lefts = [as_left(jnp.where(below, couple, 0.0)) for couple in couples]
        steps = [product(left, as_right(item)) for left, item in zip(lefts, inverse)]
        inverse = [item - product(as_left(item), as_right(step)) for item, step in zip(inverse, steps)]
        size *= 2
    results = []
    fresh_1 = [product(as_left(inverse[n]), as_right(sides[n][:HEAD])) for n in range(GROUP)]
    uses = [
        product(
            as_left(jnp.concatenate((cross[n], mix_1[n], mix_cross[n]), axis=0)), as_right(fresh_1[n])
        )
        for n in range(GROUP)
    ]
    fresh_2 = [
        product(as_left(inverse[GROUP + n]), as_right(sides[n][HEAD:] - uses[n][:HEAD]))
        for n in range(GROUP)
    ]
    for n in range(GROUP):
        second = uses[n][2 * HEAD :] + product(as_left(mix_2[n]), as_right(fresh_2[n]))
        results.append(jnp.concatenate((uses[n][HEAD : 2 * HEAD], second), axis=0))
    return results


def kernel(
    queries_hbm, keys_hbm, values_hbm, decay_hbm, strength_hbm, out_grad_hbm, weights_hbm,
    first_hbm, second_hbm, anchor_hbm, momentum_hbm, exponents,
    layer_out_hbm, state_hbm,
    queries, keys, values, decay, strength, weights, first, second, anchor, momentum,
    rows, cols, core, core_t, across_t, across_n, out_sent, out_across, core_quad, grad_quad, every_weight, partial,
    relay_up, relay_down, sum_up, sum_down, decoded, shares, halves, outer,
    load_sem, store_sem, grad_send, grad_recv, quad_send, quad_recv, row_send, row_recv,
    pair_send, pair_recv, cross_send, cross_recv, out_send, out_recv, relay_send, relay_recv, sum_send, sum_recv,
    share_send, share_recv, half_send, half_recv, outer_send, outer_recv,
):
    replica, me = lax.axis_index("replica"), lax.axis_index("fsdp")
    x, y, c = me // 8, (me // 2) % 4, me % 2

    def index(x_at, y_at, c_at):
        return x_at * 8 + lax.rem(y_at + 4, 4) * 2 + c_at

    def device(f):
        return {"replica": replica, "fsdp": f}

    sibling, across, corner = index(x, y, 1 - c), index(1 - x, y, c), index(1 - x, y, 1 - c)
    up, down = index(x, y + 1, c), index(x, y - 1, c)
    z = lax.rem(replica, 4)
    half = replica // 4
    others = [lax.rem(z + k, 4) for k in range(1, 4)]

    def replica_at(half_at, z_at):
        return {"replica": half_at * 4 + z_at, "fsdp": me}

    member = x * 2 + c
    member_sibling, member_across, member_corner = x * 2 + 1 - c, (1 - x) * 2 + c, (1 - x) * 2 + 1 - c

    started, late = [], []

    def copy(src, dst, send_sem, recv_sem, to):
        return pltpu.make_async_remote_copy(
            src_ref=src, dst_ref=dst, send_sem=send_sem, recv_sem=recv_sem,
            device_id=to, device_id_type=MESH,
        )

    def send(src, dst, send_sem, recv_sem, to, kept=started):
        item = copy(src, dst, send_sem, recv_sem, to)
        item.start()
        kept.append(item)

    def arrived(region, recv_sem):
        copy(region, region, recv_sem, recv_sem, device(sibling)).wait_recv()

    grad_own = grad_quad.at[pl.ds(pl.multiple_of(member * SEQ, SEQ), SEQ)]
    loads = [
        (weights_hbm.at[0], weights), (keys_hbm, keys), (decay_hbm, decay), (strength_hbm, strength),
        (queries_hbm, queries), (values_hbm, values), (out_grad_hbm, grad_own), (first_hbm.at[0], first),
        (second_hbm.at[0], second), (anchor_hbm, anchor), (momentum_hbm, momentum),
    ]
    loads = [pltpu.make_async_copy(src, dst, load_sem.at[n]) for n, (src, dst) in enumerate(loads)]
    barrier = pltpu.get_barrier_semaphore()
    peers = [device(f) for f in (sibling, across, corner, up, down)]
    peers += [replica_at(half, zz) for zz in others] + [replica_at(1 - half, z)]
    for peer in peers:
        pl.semaphore_signal(barrier, inc=1, device_id=peer, device_id_type=MESH)
    for load in loads[:6]:
        load.start()
    pl.semaphore_wait(barrier, len(peers))

    def weight_rows(f):
        return every_weight.at[pl.ds(pl.multiple_of(f * BLOCK, BLOCK), BLOCK)]

    def grad_part(who, j):
        return grad_quad.at[
            pl.ds(pl.multiple_of(who * SEQ, SEQ), SEQ), pl.ds(j * CHUNK, CHUNK)
        ]

    def send_grad(j):
        src = out_grad_hbm.at[:, pl.ds(j * CHUNK, CHUNK)]
        send(src, grad_part(member, j), grad_send.at[0, j], grad_recv.at[0, j], device(across))
        send(src, grad_part(member, j), grad_send.at[1, j], grad_recv.at[1, j], device(sibling))

    def pass_grad(j):
        arrived(grad_part(member_across, j), grad_recv.at[0, j])
        send(
            grad_part(member_across, j), grad_part(member_across, j),
            grad_send.at[2, j], grad_recv.at[2, j], device(sibling),
        )

    def weight_part(f, start, size):
        return every_weight.at[
            pl.ds(pl.multiple_of(f * BLOCK, BLOCK), BLOCK), pl.ds(start, size)
        ]

    def weight_piece(u, p, f):
        return weight_part(f, *PIECES[u][p])

    def weight_half(u, p, f, side):
        start, size = PIECES[u][p]
        return weight_part(f, start + side * size // 2, size // 2)

    def ring(u, p, k, f, side, to):
        part = weight_half(u, p, f, side)
        send(part, part, row_send.at[u, p, k], row_recv.at[u, p, k], device(to), (started, late)[u])

    def ring_arrived(u, p, k, f, side):
        arrived(weight_half(u, p, f, side), row_recv.at[u, p, k])

    def share_weight(u, p, k, f):
        part = weight_piece(u, p, f)
        send(part, part, pair_send.at[u, p, k], pair_recv.at[u, p, k], device(sibling), (started, late)[u])

    def cross_weight(p):
        part = weight_piece(1, p, me)
        send(part, part, cross_send.at[1 + p], cross_recv.at[1 + p], device(across))

    def take_weight(p):
        arrived(weight_piece(1, p, across), cross_recv.at[1 + p])
        ring_first(1, p, 0)
        ring_first(1, p, 1)
        share_weight(1, p, 0, across)

    column = (x, 1 - x)

    def ring_first(u, p, step):
        block = index(column[u], y, c)
        ring(u, p, 2 * step, block, step, up)
        ring(u, p, 2 * step + 1, block, 1 - step, down)

    def ring_second(u, p):
        below, above = index(column[u], y - 1, c), index(column[u], y + 1, c)
        ring_arrived(u, p, 0, below, 0)
        ring(u, p, 4, below, 0, up)
        ring_arrived(u, p, 1, above, 1)
        ring(u, p, 5, above, 1, down)

    def share_near(u, p):
        below, above = index(column[u], y - 1, c), index(column[u], y + 1, c)
        ring_arrived(u, p, 2, below, 1)
        share_weight(u, p, 1, below)
        ring_arrived(u, p, 3, above, 0)
        share_weight(u, p, 2, above)

    def share_far(u, p):
        far = index(column[u], y + 2, c)
        ring_arrived(u, p, 4, far, 0)
        ring_arrived(u, p, 5, far, 1)
        share_weight(u, p, 3, far)

    def from_sibling(u, p, k):
        shift = (0, -1, 1, 2)[k]
        arrived(weight_piece(u, p, index(column[u], y + shift, 1 - c)), pair_recv.at[u, p, k])

    for j in range(EARLY):
        send_grad(j)
    loads[0].wait()
    for p in range(2):
        start, size = PIECES[0][p]
        weight_piece(0, p, me)[...] = weights[:, start : start + size].astype(BF16)
        ring_first(0, p, 0)
        ring_first(0, p, 1)
    for p in range(2):
        share_weight(0, p, 0, me)
    for load in loads[6:]:
        load.start()

    for n in range(1, 6):
        loads[n].wait()
    fill_tables(keys, decay, strength, rows, cols)

    def heads(g, carry):
        results = delta_group(g, queries, keys, values, rows, cols)
        for n, result in enumerate(results):
            at = pl.ds(pl.multiple_of((g * GROUP + n) * HEAD, HEAD), HEAD)
            core[:, at] = result.astype(BF16)
            core_t[at, :] = result.T.astype(BF16)
        return carry

    lax.fori_loop((1 - x) * 2, (1 - x) * 2 + 2, heads, 0)
    ring_second(0, 0)
    other_rows = core_t.at[pl.ds(pl.multiple_of((1 - x) * 1024, 1024), 1024)]
    send(other_rows, across_t, cross_send.at[0], cross_recv.at[0], device(across))
    for j in range(EARLY, CHUNKS):
        send_grad(j)
    cross_weight(0)
    lax.fori_loop(x * 2, x * 2 + 2, heads, 0)
    ring_second(0, 1)

    def quad_part(who, y_at):
        return core_quad.at[
            pl.ds(pl.multiple_of(y_at * HEAD, HEAD), HEAD), pl.ds(pl.multiple_of(who * SEQ, SEQ), SEQ)
        ]

    def head_rows(ref, h):
        return ref.at[pl.ds(pl.multiple_of(h * HEAD, HEAD), HEAD)]

    def hand_out(k, ref, base, who):
        for yy in range(4):
            send(
                head_rows(ref, base + 2 * yy + 1 - c), quad_part(who, yy),
                quad_send.at[k, yy], quad_recv.at[k, yy], device(sibling),
            )
            quad_part(who, yy)[...] = head_rows(ref, base + 2 * yy + c)[...]

    hand_out(0, core_t, x * 8, member)
    arrived(across_t, cross_recv.at[0])
    hand_out(1, across_t, 0, member_across)

    def partial_at(shift, start, size):
        return partial.at[
            pl.ds(pl.multiple_of(lax.rem(y + shift + 4, 4) * BLOCK, BLOCK), BLOCK), pl.ds(start, size)
        ]

    def take_grad(j):
        arrived(grad_part(member_sibling, j), grad_recv.at[1, j])
        arrived(grad_part(member_corner, j), grad_recv.at[2, j])

    def partial_chunk(j):
        at = pl.ds(j * CHUNK, CHUNK)
        total = jnp.dot(core_quad[...], grad_quad[:, at], preferred_element_type=F32)
        partial[:, at] = (total * SCALE).astype(BF16)
        start, half = j * CHUNK, pl.ds(j * HALF, HALF)
        send(
            partial_at(2, start, HALF), relay_up.at[:, half],
            relay_send.at[0, j], relay_recv.at[0, j], device(up),
        )
        send(
            partial_at(2, start + HALF, HALF), relay_down.at[:, half],
            relay_send.at[1, j], relay_recv.at[1, j], device(down),
        )

    def relay_chunk(j):
        start, at, half = j * CHUNK, pl.ds(j * CHUNK, CHUNK), pl.ds(j * HALF, HALF)
        for shift, relay, k, place in ((1, relay_up, 0, start), (-1, relay_down, 1, start + HALF)):
            arrived(relay.at[:, half], relay_recv.at[k, j])
            spot = partial_at(shift, place, HALF)
            spot[...] = (spot[...].astype(F32) + relay[:, half].astype(F32)).astype(BF16)
        send(partial_at(1, start, CHUNK), sum_up.at[:, at], sum_send.at[0, j], sum_recv.at[0, j], device(up))
        send(partial_at(-1, start, CHUNK), sum_down.at[:, at], sum_send.at[1, j], sum_recv.at[1, j], device(down))

    power = jnp.full((1, 128), exponents[0, 0], jnp.int32).astype(F32)
    down_scale, up_scale = jnp.exp2(-power)[:, :1], jnp.exp2(power)[:, :1]

    def update_chunk(j):
        at = pl.ds(j * CHUNK, CHUNK)
        arrived(sum_up.at[:, at], sum_recv.at[0, j])
        arrived(sum_down.at[:, at], sum_recv.at[1, j])
        grad = partial_at(0, j * CHUNK, CHUNK)[...].astype(F32)
        grad = grad + sum_up[:, at].astype(F32) + sum_down[:, at].astype(F32)
        weight, base = weights[:, at], anchor[:, at]
        one = 0.9 * first[:, at] + 0.1 * grad
        two = 0.95 * second[:, at] + 0.05 * grad * grad
        updated = weight - 0.03 * (one / (jnp.sqrt(two) + 1e-08) + 0.1 * weight)
        encoded = jnp.clip((base - updated) * down_scale, -448.0, 448.0).astype(BF16)
        decoded[:, at] = (encoded.astype(F32) * up_scale).astype(BF16)
        if j % SENDS == SENDS - 1:
            group = j // SENDS
            span = pl.ds(group * SPAN, SPAN)
            for k, zz in enumerate(others):
                send(
                    decoded.at[pl.ds(pl.multiple_of(zz * SHARE, SHARE), SHARE), span], shares.at[z, :, span],
                    share_send.at[k, group], share_recv.at[z, group], replica_at(half, zz),
                )

    def share_rows(zz):
        return pl.ds(pl.multiple_of(zz * SHARE, SHARE), SHARE)

    def share_group(group):
        span = pl.ds(group * SPAN, SPAN)
        for zz in others:
            arrived(shares.at[zz, :, span], share_recv.at[zz, group])
        shares[z, :, span] = decoded[share_rows(z), span]
        total = shares[0, :, span].astype(F32)
        for zz in range(1, 4):
            total = total + shares[zz, :, span].astype(F32)
        halves[half, :, span] = total.astype(BF16)
        send(
            halves.at[half, :, span], halves.at[half, :, span],
            half_send.at[group], half_recv.at[group], replica_at(1 - half, z),
        )

    def outer_group(group):
        span = pl.ds(group * SPAN, SPAN)
        arrived(halves.at[1 - half, :, span], half_recv.at[group])
        total = halves[0, :, span].astype(F32) + halves[1, :, span].astype(F32)
        outer[share_rows(z), span] = (total * (1.0 / REPLICAS)).astype(BF16)
        part = outer.at[share_rows(z), span]
        for k, zz in enumerate(others):
            send(part, part, outer_send.at[k, group], outer_recv.at[z, group], replica_at(half, zz), late)

    def product_across():
        for h in range(8):
            across_n[:, h * HEAD : (h + 1) * HEAD] = (
                across_t[h * HEAD : (h + 1) * HEAD, :].astype(F32).T.astype(BF16)
            )

        def tile(n, carry):
            at = pl.multiple_of(n * TILE, TILE)
            total = jnp.dot(
                across_n[...],
                every_weight[pl.ds(pl.multiple_of(x * 1024, 1024), 1024), pl.ds(WHOLE + at, TILE)],
                preferred_element_type=F32,
            )
            out_sent[:, pl.ds(at, TILE)] = (total * SCALE).astype(BF16)
            return carry

        lax.fori_loop(0, SHARED // TILE, tile, 0)

    def send_product(k):
        start, size = OUTS[1 + k]
        at = pl.ds(start - WHOLE, size)
        send(out_sent.at[:, at], out_across.at[:, at], out_send.at[k], out_recv.at[k], device(across), late)

    for j in range(EARLY):
        pass_grad(j)
    for n in range(6, 11):
        loads[n].wait()
    for yy in range(4):
        arrived(quad_part(member_sibling, yy), quad_recv.at[0, yy])
        arrived(quad_part(member_corner, yy), quad_recv.at[1, yy])

    for j in range(CHUNKS):
        take_grad(j)
        partial_chunk(j)
        if j >= 2:
            update_chunk(j - 2)
        if j >= 1:
            relay_chunk(j - 1)
        if EARLY <= j + 1 < CHUNKS:
            pass_grad(j + 1)
        if j == 2:
            share_near(0, 0)
            share_near(0, 1)
        if j == 3:
            share_far(0, 0)
            share_far(0, 1)
        if j == 4:
            for k in range(4):
                from_sibling(0, 1, k)
            product_across()
            send_product(0)
        if j >= 6:
            share_group(j - 6)
    relay_chunk(CHUNKS - 1)
    update_chunk(CHUNKS - 2)
    share_group(2)
    update_chunk(CHUNKS - 1)
    take_weight(0)
    share_group(3)
    for k in range(1, 4):
        send_product(k)
    for group in range(3):
        outer_group(group)

    def multiply(tiles, spots, size, begin, finish):
        def tile(n, carry):
            at = pl.ds(pl.multiple_of(n * TILE, TILE), TILE)
            total = None
            for spot in spots:
                term = jnp.dot(
                    core[:, pl.ds(spot, size)], every_weight[pl.ds(spot, size), at],
                    preferred_element_type=F32,
                )
                total = term if total is None else total + term
            if not begin:
                total = total + jnp.concatenate((first[:, at], second[:, at]), axis=0)
            if finish:
                partial[0:SEQ, at] = (total * SCALE).astype(BF16)
            else:
                first[:, at] = total[:BLOCK]
                second[:, at] = total[BLOCK:]
            return carry

        lax.fori_loop(tiles[0], tiles[1], tile, 0)

    def store_out(k):
        start, size = OUTS[k]
        at = pl.ds(start, size)
        store = pltpu.make_async_copy(partial.at[0:SEQ, at], layer_out_hbm.at[:, at], store_sem.at[k])
        store.start()
        stores.append(store)

    def add_across(k):
        start, size = OUTS[1 + k]
        part, at = pl.ds(start - WHOLE, size), pl.ds(start, size)
        arrived(out_across.at[:, part], out_recv.at[k])
        for ref, spot in ((first, pl.ds(0, BLOCK)), (second, pl.ds(BLOCK, BLOCK))):
            partial[spot, at] = (ref[:, at] * SCALE + out_across[spot, part].astype(F32)).astype(BF16)
        store_out(1 + k)

    def outer_step(zz):
        spot = share_rows(zz)
        delta = outer[spot, :].astype(F32)
        moved = 0.9 * momentum[spot, :] + delta
        momentum[spot, :] = moved
        anchor[spot, :] = anchor[spot, :] - 0.7 * (delta + 0.9 * moved)

    stores = []
    for k in range(4):
        from_sibling(0, 0, k)
    multiply((0, D // TILE), [pl.multiple_of(x * 1024, 1024)], 1024, True, False)
    ring_second(1, 0)
    outer_group(3)
    for item in started:
        item.wait_send()
    outer_step(z)
    for zz in others:
        for group in range(CHUNKS // SENDS):
            arrived(outer.at[share_rows(zz), pl.ds(group * SPAN, SPAN)], outer_recv.at[zz, group])
        outer_step(zz)
    for n, ref in enumerate((anchor, momentum)):
        store = pltpu.make_async_copy(ref, state_hbm.at[n * BLOCK : (n + 1) * BLOCK], store_sem.at[6 + n])
        store.start()
        stores.append(store)
    share_near(1, 0)
    share_far(1, 0)
    for k in range(4):
        from_sibling(1, 0, k)
    multiply((0, WHOLE // TILE), [pl.multiple_of((1 - x) * 1024, 1024)], 1024, False, True)
    store_out(0)
    for k in range(4):
        add_across(k)
    for item in late:
        item.wait_send()
    for store in stores:
        store.wait()


def on_device(
    queries, keys, values, log_decay, write_strength, out_grad, replica_weights,
    adam_first, adam_second, anchor, outer_momentum, exponents,
):
    dma = pltpu.SemaphoreType.DMA
    scratch = [
        pltpu.VMEM((SEQ, WIDTH), BF16),
        pltpu.VMEM((SEQ, WIDTH), BF16),
        pltpu.VMEM((SEQ, WIDTH), BF16),
        pltpu.VMEM((HEADS, SEQ), F32),
        pltpu.VMEM((HEADS, SEQ), F32),
        pltpu.VMEM((BLOCK, D), F32),
        pltpu.VMEM((BLOCK, D), F32),
        pltpu.VMEM((BLOCK, D), F32),
        pltpu.VMEM((BLOCK, D), F32),
        pltpu.VMEM((BLOCK, D), F32),
        pltpu.VMEM((GROUPS, 128, SEQ), F32),
        pltpu.VMEM((GROUPS, SEQ, 128), F32),
        pltpu.VMEM((SEQ, WIDTH), BF16),
        pltpu.VMEM((WIDTH, SEQ), BF16),
        pltpu.VMEM((WIDTH // 2, SEQ), BF16),
        pltpu.VMEM((SEQ, WIDTH // 2), BF16),
        pltpu.VMEM((SEQ, SHARED), BF16),
        pltpu.VMEM((SEQ, SHARED), BF16),
        pltpu.VMEM((4 * HEAD, 4 * SEQ), BF16),
        pltpu.VMEM((4 * SEQ, D), BF16),
        pltpu.VMEM((WIDTH, D), BF16),
        pltpu.VMEM((4 * BLOCK, D), BF16),
        pltpu.VMEM((BLOCK, SIDE), BF16),
        pltpu.VMEM((BLOCK, SIDE), BF16),
        pltpu.VMEM((BLOCK, D), BF16),
        pltpu.VMEM((BLOCK, D), BF16),
        pltpu.VMEM((BLOCK, D), BF16),
        pltpu.VMEM((4, SHARE, D), BF16),
        pltpu.VMEM((2, SHARE, D), BF16),
        pltpu.VMEM((BLOCK, D), BF16),
        dma((11,)), dma((8,)),
        dma((3, CHUNKS)), dma((3, CHUNKS)),
        dma((2, 4)), dma((2, 4)),
        dma((2, 2, 6)), dma((2, 2, 6)),
        dma((2, 2, 4)), dma((2, 2, 4)),
        dma((3,)), dma((3,)),
        dma((4,)), dma((4,)),
        dma((2, CHUNKS)), dma((2, CHUNKS)),
        dma((2, CHUNKS)), dma((2, CHUNKS)),
        dma((3, 4)), dma((4, 4)),
        dma((4,)), dma((4,)),
        dma((3, 4)), dma((4, 4)),
    ]
    anywhere = pl.BlockSpec(memory_space=pl.ANY)
    layer_out, state = pl.pallas_call(
        kernel,
        out_shape=(
            jax.ShapeDtypeStruct((SEQ, D), BF16),
            jax.ShapeDtypeStruct((2 * BLOCK, D), F32),
        ),
        in_specs=[anywhere] * 11 + [pl.BlockSpec(memory_space=pltpu.SMEM)],
        out_specs=(anywhere,) * 2,
        scratch_shapes=scratch,
        compiler_params=pltpu.CompilerParams(
            collective_id=0, has_side_effects=True, vmem_limit_bytes=60 * 1024 * 1024
        ),
        name="diloco_step",
    )(
        queries, keys, values, log_decay, write_strength, out_grad, replica_weights,
        adam_first, adam_second, anchor, outer_momentum, exponents,
    )
    return layer_out, state[:BLOCK], state[BLOCK:]


def solution(mesh):
    return jax.shard_map(
        on_device,
        mesh=mesh,
        in_specs=(
            P(("replica", "fsdp"), None),
            P(("replica", "fsdp"), None),
            P(("replica", "fsdp"), None),
            P(None, ("replica", "fsdp")),
            P(None, ("replica", "fsdp")),
            P(("replica", "fsdp"), None),
            P("replica", "fsdp", None),
            P("replica", "fsdp", None),
            P("replica", "fsdp", None),
            P("fsdp", None),
            P("fsdp", None),
            P("replica", "fsdp"),
        ),
        out_specs=(P(("replica", "fsdp"), None), P("fsdp", None), P("fsdp", None)),
        check_vma=False,
    )
```
